512 devices in a mesh: mem: 16 (over y_lo, x, core), sp: 32 (over y_hi, z).
Axes of the slice: x: 4, y: 4 (y_hi: 2, y_lo: 2; y = y_hi * 2 + y_lo), z: 16, core: 2. Of those that a mesh axis runs over, the one named last changes fastest.
Arguments:
- cycle_start_state: float32 [128, 3, 6, 24576], P('mem', None, None, 'sp'), may hold values from -6 to 6
- diffusivity: float32 [6], replicated, may hold values from 0.04 to 0.22
- coupling: float32 [3, 3], replicated, may hold values from -0.3 to 0.3
- observation_value: float32 [32, 16, 512], P('sp', 'mem'), may hold values from -8 to 8
- observation_cell: int32 [32, 16, 512], P('sp', 'mem'), may hold values from 0 to 863
- observation_lists: int32 [32, 16, 8, 256], P('sp', 'mem'), may hold values from 0 to 511
- localization_weight: float32 [32, 16, 8, 256], P('sp', 'mem'), may hold values from 0.2 to 2
Outputs:
- analysis: float32 [128, 3, 6, 24576], P('mem', None, None, 'sp')
The draws below stay inside these ranges and needn't reach their ends.
Inputs may be any that keep to these rules, and one draw needn't show every extreme that they name: `observation_cell`: index into one member's 864 values of tile (a, b), ordered field, level, row, column. `observation_lists`: index into the 512 observations of the same tile; repeats possible.
All inputs are finite; a program needn't handle non-finite values.
Results may differ from the reference program's by a relative error of at most 0.0003.
Values sent between devices are 32-bit elements; how exact they have to be, the bound alone decides.
A program may use at most 64 MiB of HBM per device.

```python
import math
import jax
import jax.numpy as jnp
from jax import lax

PATCH_NORTHWARD = 4
DOMAIN_COLUMNS = 192
VERTICAL_LAYERS = 6
PROGNOSTIC_VARS = 3
NOBS = 512
NLOC = 256
GX = 4
GY = 2
ENSEMBLE_SIZE = 128
DOMAIN_ROWS = 128
PATCH_EASTWARD = 12
CELLS = 864
TILES_Y = 32
TILES_X = 16


def place_ends(array, stream_key, smallest, largest):
    index_at = [jax.random.randint(jax.random.fold_in(stream_key, axis), (), 0, length) for axis, length in enumerate(array.shape)]
    longest = array.shape.index(max(array.shape))
    next_to = index_at[:longest] + [(index_at[longest] + 1) % array.shape[longest]] + index_at[longest + 1:]
    return array.at[tuple(index_at)].set(smallest).at[tuple(next_to)].set(largest)


def level_of(key, extent, split, low, largest):
    loudness, own = 1.0, jax.random.fold_in(key, 6)
    for dim, parts in split:
        draws = jnp.exp(jax.random.uniform(jax.random.fold_in(own, dim), (parts,), jnp.float32, low / len(split), largest / len(split)))
        loudness = loudness * jnp.repeat(draws, extent[dim] // parts).reshape([-1 if axis == dim else 1 for axis in range(len(extent))])
    return loudness


def centred(stream_key, shape, scale, limit, pieces=(), held_as=jnp.bfloat16):
    values = jax.random.normal(stream_key, shape, jnp.float32) * scale
    if len(pieces) > 0:
        values = level_of(stream_key, shape, pieces, -0.22, 0.18) * values
    return jnp.clip(values, min=-limit, max=limit).astype(held_as)


def setup_inputs(seed: int = 0) -> dict:
    key_of = jax.random.split(jax.random.key(seed), 8)
    return {
        "cycle_start_state": centred(key_of[0], (ENSEMBLE_SIZE, PROGNOSTIC_VARS, VERTICAL_LAYERS, DOMAIN_ROWS * DOMAIN_COLUMNS), 1.0, 6.0, ((0, 16), (3, 32)), jnp.float32),
        "diffusivity": jnp.clip(jnp.exp(jax.random.uniform(key_of[1], (VERTICAL_LAYERS,), jnp.float32, math.log(0.04), math.log(0.22))), 0.04, 0.22),
        "coupling": jnp.clip(jax.random.uniform(key_of[2], (PROGNOSTIC_VARS, PROGNOSTIC_VARS), jnp.float32, -0.3, 0.3), -0.3, 0.3),
        "observation_value": centred(key_of[3], (TILES_Y, TILES_X, NOBS), 1.5, 8.0, ((0, 32), (1, 16)), jnp.float32),
        "observation_cell": place_ends(jax.random.randint(key_of[4], (TILES_Y, TILES_X, NOBS), 0, CELLS), jax.random.fold_in(key_of[4], 1), 0, CELLS - 1).astype(jnp.int32),
        "observation_lists": place_ends(jax.random.randint(key_of[5], (TILES_Y, TILES_X, GX * GY, NLOC), 0, NOBS), jax.random.fold_in(key_of[5], 1), 0, NOBS - 1).astype(jnp.int32),
        "localization_weight": jnp.clip(jnp.exp(math.log(2.0) - 2.3025851 * jax.random.uniform(key_of[6], (TILES_Y, TILES_X, GX * GY, NLOC), jnp.float32) ** level_of(key_of[6], (TILES_Y, TILES_X, GX * GY, NLOC), ((0, 32), (1, 16)), -0.2, 0.2)), 0.2, 2.0),
    }


def advance(extended, diffusivity, coupling):
    center = extended[..., 1:-1, :]
    widths = [(0, 0)] * (center.ndim - 1) + [(1, 1)]
    sides = jnp.pad(center, widths)
    laplace = extended[..., 2:, :] + extended[..., :-2, :] + sides[..., 2:] + sides[..., :-2] - 4.0 * center
    mixing = jnp.einsum('fg,...glyx->...flyx', coupling, center, precision=lax.Precision.HIGHEST)
    return center + diffusivity[:, None, None] * laplace + mixing

def hat_table(row_stack, cols):
    row_pos = jnp.arange(row_stack, dtype=jnp.float32)
    col_pos = jnp.arange(cols, dtype=jnp.float32)
    span_y = (row_stack - 1) / (GY - 1)
    span_x = (cols - 1) / (GX - 1)
    centre_y = jnp.arange(GY, dtype=jnp.float32) * span_y
    centre_x = jnp.arange(GX, dtype=jnp.float32) * span_x
    hat_y = jnp.maximum(0.0, 1.0 - jnp.abs(row_pos[None, :] - centre_y[:, None]) / span_y)
    hat_x = jnp.maximum(0.0, 1.0 - jnp.abs(col_pos[None, :] - centre_x[:, None]) / span_x)
    hats = hat_y[:, None, :, None] * hat_x[None, :, None, :]
    return hats.reshape(GY * GX, row_stack * cols)

def lower_solve(factor, rhs, flipped):
    return lax.linalg.triangular_solve(factor, rhs, left_side=True, lower=True, transpose_a=flipped)

def coarse_weights(ens_values, observed, chosen_lists, scale_lists):
    members = ens_values.shape[0]
    ens_mean = lax.optimization_barrier(jnp.mean(ens_values, axis=0))
    perturbed = ens_values - ens_mean
    departure = observed - ens_mean
    identity = jnp.eye(members, dtype=jnp.float32)

    def single_point(chosen, scales):
        near = jnp.take(perturbed, chosen, axis=1)
        scaled = near * scales[None, :]
        precision_matrix = jnp.dot(scaled, near.T, precision=lax.Precision.HIGHEST) + (members - 1.0) * identity
        factor = jnp.linalg.cholesky(precision_matrix)
        pull = jnp.dot(scaled, jnp.take(departure, chosen), precision=lax.Precision.HIGHEST)
        middle = lower_solve(factor, pull[:, None], False)
        mean_weight = lower_solve(factor, middle, True)[:, 0]
        spread = lower_solve(factor, jnp.sqrt(members - 1.0) * identity, True)
        return spread + mean_weight[:, None]
    return jax.vmap(single_point)(chosen_lists, scale_lists)

def analyse_tile(patch_portion, observed, cells, chosen_lists, scale_lists):
    members = patch_portion.shape[0]
    flat = patch_portion.reshape(members, -1)
    weights = coarse_weights(jnp.take(flat, cells, axis=1), observed, chosen_lists, scale_lists)
    column_mean = lax.optimization_barrier(jnp.mean(flat, axis=0))
    deviation = (flat - column_mean).reshape(members, PROGNOSTIC_VARS * VERTICAL_LAYERS, PATCH_NORTHWARD * PATCH_EASTWARD)
    hats = hat_table(PATCH_NORTHWARD, PATCH_EASTWARD)
    per_column = jnp.einsum('cq,ckj->qkj', hats, weights, precision=lax.Precision.HIGHEST)
    moved = jnp.einsum('qkj,kvq->jvq', per_column, deviation, precision=lax.Precision.HIGHEST)
    return column_mean.reshape(PROGNOSTIC_VARS * VERTICAL_LAYERS, PATCH_NORTHWARD * PATCH_EASTWARD) + moved

def reference(cycle_start_state, diffusivity, coupling, observation_value, observation_cell, observation_lists, localization_weight):
    gridded_prognostics = cycle_start_state.reshape(ENSEMBLE_SIZE, PROGNOSTIC_VARS, VERTICAL_LAYERS, DOMAIN_ROWS, DOMAIN_COLUMNS)

    def ensemble_prediction(ensemble_trajectory):
        for step in range(2):
            extended = jnp.pad(ensemble_trajectory, ((0, 0), (0, 0), (1, 1), (0, 0)))
            ensemble_trajectory = advance(extended, diffusivity, coupling)
        return ensemble_trajectory
    predictive_integration = lax.map(ensemble_prediction, gridded_prognostics)
    owners = TILES_Y * TILES_X

    def owner_step(inputs):
        owner, observed, cells, chosen_lists, scale_lists = inputs
        patch_northward_position = (owner // TILES_X).astype(jnp.int32)
        patch_eastward_position = (owner % TILES_X).astype(jnp.int32)
        additive_neutral = jnp.int32(0)
        patch_portion = lax.dynamic_slice(predictive_integration, (additive_neutral, additive_neutral, additive_neutral, patch_northward_position * PATCH_NORTHWARD, patch_eastward_position * PATCH_EASTWARD), (ENSEMBLE_SIZE, PROGNOSTIC_VARS, VERTICAL_LAYERS, PATCH_NORTHWARD, PATCH_EASTWARD))
        return analyse_tile(patch_portion, observed, cells, chosen_lists, scale_lists)
    stacked = lax.map(owner_step, (jnp.arange(owners, dtype=jnp.int32), observation_value.reshape(owners, NOBS), observation_cell.reshape(owners, NOBS), observation_lists.reshape(owners, GX * GY, NLOC), localization_weight.reshape(owners, GX * GY, NLOC)))
    stacked = stacked.reshape(TILES_Y, TILES_X, ENSEMBLE_SIZE, PROGNOSTIC_VARS, VERTICAL_LAYERS, PATCH_NORTHWARD, PATCH_EASTWARD)
    return jnp.transpose(stacked, (2, 3, 4, 0, 5, 1, 6)).reshape(ENSEMBLE_SIZE, PROGNOSTIC_VARS, VERTICAL_LAYERS, DOMAIN_ROWS * DOMAIN_COLUMNS)
```

```python
import jax
import jax.numpy as jnp
from jax import lax
from jax.experimental import pallas as pl
from jax.experimental.pallas import tpu as pltpu
from jax.sharding import PartitionSpec as P

COARSE = 8
PIVOTS = 8
F32 = jnp.float32
BF16 = jnp.bfloat16
NT = (((1,), (1,)), ((), ()))
NN = (((1,), (0,)), ((), ()))


def dot(a, b, dims):
    return lax.dot_general(a, b, dims, preferred_element_type=F32)


def split2(x):
    hi = x.astype(BF16)
    lo = (x - hi.astype(F32)).astype(BF16)
    return hi, lo


def split3(x):
    hi = x.astype(BF16)
    rest = x - hi.astype(F32)
    mid = rest.astype(BF16)
    lo = (rest - mid.astype(F32)).astype(BF16)
    return hi, mid, lo


def observation_sums(lists, scales, observed, cells, lanes):
    nobs = observed.shape[1]
    points, nloc = lists.shape
    pieces = jnp.concatenate(split3(scales), axis=0)
    which = lax.broadcasted_iota(jnp.int32, (nobs, nloc), 0)
    row = lax.broadcasted_iota(jnp.int32, (points, nobs), 0)
    per_obs = jnp.zeros((points, nobs), F32)
    for c in range(points):
        picked = jnp.where(lists[c : c + 1, :] == which, 1.0, 0.0).astype(BF16)
        got = dot(pieces, picked, NT)
        got = got[:points] + got[points : 2 * points] + got[2 * points :]
        per_obs = jnp.where(row == c, got, per_obs)
    both = jnp.concatenate(split3(per_obs) + split3(per_obs * observed), axis=0)
    place = lax.broadcasted_iota(jnp.int32, (lanes, nobs), 0)
    spots = jnp.where(cells == place, 1.0, 0.0).astype(BF16)
    got = dot(both, spots, NT)
    p = points
    weight = got[:p] + got[p : 2 * p] + got[2 * p : 3 * p]
    total = got[3 * p : 4 * p] + got[4 * p : 5 * p] + got[5 * p :]
    return weight, total


def factor_inverses(r_ref, members):
    p = COARSE
    lane = lax.broadcasted_iota(jnp.int32, (p, members), 1)

    def spread(v, i):
        return jnp.broadcast_to(v[:, i : i + 1], v.shape)

    for k0 in range(0, members, PIVOTS):
        rows = [r_ref[pl.ds(p * (k0 + t), p), :] for t in range(PIVOTS)]
        done = []
        for t in range(PIVOTS):
            k = k0 + t
            pivot = spread(rows[t], k)
            own = jnp.where(lane == k, 1.0, rows[t])
            unit = own * (1.0 / pivot)
            for s in range(t + 1, PIVOTS):
                rows[s] = jnp.where(lane == k, 0.0, rows[s]) - spread(rows[t], k0 + s) * unit
            done.append(own * lax.rsqrt(pivot))
        for t in range(PIVOTS):
            r_ref[pl.ds(p * (k0 + t), p), :] = jnp.where(lane <= k0 + t, done[t], 0.0)
        block = (lane >= k0) & (lane < k0 + PIVOTS)
        kept = [jnp.where(block & (lane > k0 + t), 0.0, done[t]) for t in range(PIVOTS)]
        for i in range(k0 + PIVOTS, members):
            acc = jnp.where(block, 0.0, r_ref[pl.ds(p * i, p), :])
            for t in range(PIVOTS):
                acc = acc - spread(done[t], i) * kept[t]
            r_ref[pl.ds(p * i, p), :] = acc


def analysis_kernel(field_ref, lists_ref, scales_ref, observed_ref, cells_ref, hats_ref, out_ref, r_ref):
    members, lanes = field_ref.shape
    p = COARSE
    weight, total = observation_sums(lists_ref[...], scales_ref[...], observed_ref[...], cells_ref[...], lanes)
    field = field_ref[...]
    mean = jnp.sum(field, axis=0, keepdims=True) * (1.0 / members)
    dev = field - mean
    hi, lo = split2(dev)
    lead = float(members - 1)
    eye = jnp.where(
        lax.broadcasted_iota(jnp.int32, (members, members), 0) == lax.broadcasted_iota(jnp.int32, (members, members), 1),
        lead,
        0.0,
    )
    for c in range(p):
        s_hi, s_lo = split2(dev * weight[c : c + 1, :])
        g = dot(s_hi, hi, NT) + dot(s_hi, lo, NT) + dot(s_lo, hi, NT) + eye
        r_ref[pl.ds(c, members, stride=p), :] = g
    gap = total - mean * weight
    g_hi, g_lo = split2(gap)
    pull = dot(g_hi, hi, NT) + dot(g_hi, lo, NT) + dot(g_lo, hi, NT)

    factor_inverses(r_ref, members)

    root = lead**0.5
    moved = jnp.zeros((members, lanes), F32)
    for c in range(p):
        m = r_ref[pl.ds(c, members, stride=p), :]
        y = lax.dot_general(pull[c : c + 1, :], m, NT, precision=lax.Precision.HIGHEST, preferred_element_type=F32)
        w = lax.dot_general(y, m, NN, precision=lax.Precision.HIGHEST, preferred_element_type=F32)
        w_hi, w_lo = split2(m * root + w)
        moved = moved + hats_ref[c : c + 1, :] * (dot(w_hi, hi, NN) + dot(w_hi, lo, NN) + dot(w_lo, hi, NN))
    out_ref[...] = mean + moved


def analyse(field, lists, scales, observed, cells, hats):
    members, lanes = field.shape
    return pl.pallas_call(
        analysis_kernel,
        out_shape=jax.ShapeDtypeStruct((members, lanes), F32),
        in_specs=[pl.BlockSpec(memory_space=pltpu.VMEM)] * 6,
        out_specs=pl.BlockSpec(memory_space=pltpu.VMEM),
        scratch_shapes=[pltpu.VMEM((COARSE * members, members), F32)],
        compiler_params=pltpu.CompilerParams(vmem_limit_bytes=48 * 1024 * 1024),
    )(field, lists, scales, observed, cells, hats)


DOMAIN_COLUMNS = 192
GX = 4
GY = 2


def padded(x, sides, width):
    for axis, dim in sides:
        count, length = (lax.axis_size(axis), x.shape[dim])
        up = [(i, (i + 1) % count) for i in range(count - 1)]
        down = [(j, i) for i, j in up]
        last = lax.slice_in_dim(x, length - width, length, axis=dim)
        first = lax.slice_in_dim(x, 0, width, axis=dim)
        before = lax.ppermute(last, axis, up)
        after = lax.ppermute(first, axis, down)
        x = jnp.concatenate([before, x, after], axis=dim)
    return x


def advance(extended, diffusivity, coupling):
    center = extended[..., 1:-1, :]
    widths = [(0, 0)] * (center.ndim - 1) + [(1, 1)]
    sides = jnp.pad(center, widths)
    laplace = (
        extended[..., 2:, :]
        + extended[..., :-2, :]
        + sides[..., 2:]
        + sides[..., :-2]
        - 4.0 * center
    )
    mixing = jnp.einsum("fg,...glyx->...flyx", coupling, center, precision=lax.Precision.HIGHEST)
    return center + diffusivity[:, None, None] * laplace + mixing


def hat_table(row_stack, cols):
    row_pos = jnp.arange(row_stack, dtype=jnp.float32)
    col_pos = jnp.arange(cols, dtype=jnp.float32)
    span_y = (row_stack - 1) / (GY - 1)
    span_x = (cols - 1) / (GX - 1)
    centre_y = jnp.arange(GY, dtype=jnp.float32) * span_y
    centre_x = jnp.arange(GX, dtype=jnp.float32) * span_x
    hat_y = jnp.maximum(0.0, 1.0 - jnp.abs(row_pos[None, :] - centre_y[:, None]) / span_y)
    hat_x = jnp.maximum(0.0, 1.0 - jnp.abs(col_pos[None, :] - centre_x[:, None]) / span_x)
    hats = hat_y[:, None, :, None] * hat_x[None, :, None, :]
    return hats.reshape(GY * GX, row_stack * cols)


def on_device(
    cycle_start_state,
    diffusivity,
    coupling,
    observation_value,
    observation_cell,
    observation_lists,
    localization_weight,
):
    member_group = cycle_start_state.shape[0]
    field_stack = cycle_start_state.shape[1]
    local_levels = cycle_start_state.shape[2]
    width_span = DOMAIN_COLUMNS
    row_stack = cycle_start_state.shape[3] // width_span
    tiles = lax.axis_size("mem")
    tile_cols = width_span // tiles
    ensemble_trajectory = cycle_start_state
    for step in range(2):
        extended = padded(ensemble_trajectory, (("sp", 3),), DOMAIN_COLUMNS)
        grid_ext = extended.reshape(
            member_group, field_stack, local_levels, row_stack + 2, width_span
        )
        ensemble_trajectory = advance(grid_ext, diffusivity, coupling).reshape(
            ensemble_trajectory.shape
        )
    level_stack = field_stack * local_levels
    hats = hat_table(row_stack, tile_cols)
    layered = ensemble_trajectory.reshape(member_group, level_stack, row_stack, width_span)
    columns = lax.all_to_all(layered, "mem", split_axis=3, concat_axis=0, tiled=True)
    members = columns.shape[0]
    flat = columns.reshape(members, -1)
    cells = flat.shape[1]
    padded_cells = -cells % 128
    analysed = analyse(
        jnp.pad(flat, ((0, 0), (0, padded_cells))),
        observation_lists[0, 0],
        localization_weight[0, 0],
        observation_value[0],
        observation_cell[0],
        jnp.pad(jnp.tile(hats, (1, level_stack)), ((0, 0), (0, padded_cells))),
    )[:, :cells].reshape(columns.shape)
    result_state = lax.all_to_all(analysed, "mem", split_axis=0, concat_axis=3, tiled=True)
    return result_state.reshape(cycle_start_state.shape)


def solution(mesh):
    in_specs = (
        P("mem", None, None, "sp"),
        P(),
        P(),
        P("sp", "mem", None),
        P("sp", "mem", None),
        P("sp", "mem", None, None),
        P("sp", "mem", None, None),
    )
    out_specs = P("mem", None, None, "sp")
    return jax.shard_map(
        on_device, mesh=mesh, in_specs=in_specs, out_specs=out_specs, check_vma=False
    )
```

```python
import functools

import jax
import jax.numpy as jnp
from jax import lax
from jax.experimental import pallas as pl
from jax.experimental.pallas import tpu as pltpu
from jax.sharding import PartitionSpec as P

GX = 4
GY = 2
COARSE = 8
PIVOTS = 8
F32 = jnp.float32
BF16 = jnp.bfloat16
NT = (((1,), (1,)), ((), ()))
NN = (((1,), (0,)), ((), ()))
MESH = pl.DeviceIdType.MESH
LANES = 128
TILE_COLS = 12
HALF = 96


def lane_ids(shape):
    return lax.broadcasted_iota(jnp.int32, shape, len(shape) - 1)


def turn(x, shift):
    return pltpu.roll(x, shift % LANES, x.ndim - 1)


def swap_blocks(rows):
    rows = list(rows)
    lane = lane_ids(rows[0].shape)
    for step in (4, 2, 1):
        width = TILE_COLS * step
        keep = lane % (2 * width) < width
        for a in range(8):
            if a & step:
                continue
            low, high = rows[a], rows[a + step]
            rows[a] = jnp.where(keep, low, turn(high, width))
            rows[a + step] = jnp.where(keep, turn(low, -width), high)
    return rows


def pack_four(parts):
    lane = lane_ids(parts[0].shape)
    one, two, three = turn(parts[1], 96), turn(parts[2], 64), turn(parts[3], 32)
    return [
        jnp.where(lane < 96, parts[0], one),
        jnp.where(lane < 64, one, two),
        jnp.where(lane < 32, two, three),
    ]


def unpack_four(vecs):
    lane = lane_ids(vecs[0].shape)
    return [
        vecs[0],
        turn(jnp.where(lane < 64, vecs[1], vecs[0]), -96),
        turn(jnp.where(lane < 64, vecs[2], vecs[1]), -64),
        turn(vecs[2], -32),
    ]


def row_halves(vecs):
    lane = lane_ids(vecs[0].shape)
    first, middle, last = vecs
    return [
        (first, jnp.where(lane < 64, middle, first)),
        (turn(jnp.where(lane < 64, last, middle), 64), turn(last, 64)),
    ]


def time_step(rows, diffusion, mix):
    fields, count = len(rows), len(rows[0])
    lane = lane_ids(rows[0][0][0].shape)
    out = [[None] * (count - 2) for _ in range(fields)]
    for r in range(1, count - 1):
        pair = [[None, None] for _ in range(fields)]
        for h in range(2):
            for f in range(fields):
                center = rows[f][r][h]
                before, after = turn(center, 1), turn(center, -1)
                if h == 0:
                    before = jnp.where(lane == 0, 0.0, before)
                else:
                    after = jnp.where(lane == 63, 0.0, after)
                around = (rows[f][r - 1][h] + rows[f][r + 1][h]) + (before + after)
                new = diffusion * around
                for g in range(fields):
                    new = new + mix[f][g] * rows[g][r][h]
                pair[f][h] = new
        for f in range(fields):
            out[f][r - 1] = tuple(pair[f])
    return out


def greet(axis_sizes, partners):
    barrier = pltpu.get_barrier_semaphore()
    mem, sp = lax.axis_index("mem"), lax.axis_index("sp")
    tiles, bands = axis_sizes

    @pl.loop(1, tiles)
    def _(j):
        pl.semaphore_signal(barrier, inc=1, device_id={"mem": lax.rem(mem + j, tiles)}, device_id_type=MESH)

    if partners:

        @pl.when(sp > 0)
        def _():
            pl.semaphore_signal(barrier, inc=1, device_id={"sp": sp - 1}, device_id_type=MESH)

        @pl.when(sp < bands - 1)
        def _():
            pl.semaphore_signal(barrier, inc=1, device_id={"sp": sp + 1}, device_id_type=MESH)


def await_greetings(axis_sizes, partners):
    sp = lax.axis_index("sp")
    tiles, bands = axis_sizes
    count = tiles - 1
    if partners:
        count = count + jnp.minimum(sp, 1) + jnp.minimum(bands - 1 - sp, 1)
    pl.semaphore_wait(pltpu.get_barrier_semaphore(), count)


def forecast_kernel(
    axis_sizes, fields, levels, x_ref, diffusion_ref, coupling_ref, out_ref,
    north, south, grown, blocks, packed, landed, halo_send, halo_recv, block_send, block_recv,
):
    mem, sp = lax.axis_index("mem"), lax.axis_index("sp")
    tiles, bands = axis_sizes
    layers = fields * levels
    groups = layers // 2
    two = 3 * LANES

    greet(axis_sizes, True)
    await_greetings(axis_sizes, True)

    down = pltpu.make_async_remote_copy(
        src_ref=x_ref.at[:, :, pl.ds(two, two)], dst_ref=north, send_sem=halo_send.at[0], recv_sem=halo_recv.at[0],
        device_id={"sp": lax.rem(sp + 1, bands)}, device_id_type=MESH,
    )
    up = pltpu.make_async_remote_copy(
        src_ref=x_ref.at[:, :, pl.ds(0, two)], dst_ref=south, send_sem=halo_send.at[1], recv_sem=halo_recv.at[1],
        device_id={"sp": lax.rem(sp + bands - 1, bands)}, device_id_type=MESH,
    )

    @pl.when(sp < bands - 1)
    def _():
        down.start()

    @pl.when(sp > 0)
    def _():
        up.start()

    @pl.when(sp == 0)
    def _():
        north[...] = jnp.zeros_like(north)

    @pl.when(sp == bands - 1)
    def _():
        south[...] = jnp.zeros_like(south)

    @pl.when(sp > 0)
    def _():
        down.wait_recv()

    @pl.when(sp < bands - 1)
    def _():
        up.wait_recv()

    inside_north = jnp.minimum(sp, 1).astype(F32)
    inside_south = jnp.minimum(bands - 1 - sp, 1).astype(F32)

    @pl.loop(0, levels)
    def _(level):
        diffusion = diffusion_ref[level]
        own = 1.0 - 4.0 * diffusion
        mix = [[coupling_ref[f, g] + own if f == g else coupling_ref[f, g] for g in range(fields)] for f in range(fields)]
        rows = []
        for f in range(fields):
            layer = f * levels + level
            line = []
            for ref, starts in ((north, (0,)), (x_ref, (0, two)), (south, (0,))):
                for start in starts:
                    line += row_halves([ref[layer, :, pl.ds(start + LANES * v, LANES)] for v in range(3)])
            rows.append(line)
        middle = time_step(rows, diffusion, mix)
        for f in range(fields):
            middle[f][0] = tuple(inside_north * v for v in middle[f][0])
            middle[f][-1] = tuple(inside_south * v for v in middle[f][-1])
        final = time_step(middle, diffusion, mix)
        for f in range(fields):
            layer = f * levels + level
            for r in range(len(final[f])):
                grown[0, layer, r] = final[f][r][0]
                grown[1, layer, r] = turn(final[f][r][1], 32)

    for half in range(2):

        @pl.loop(0, groups)
        def _(group):
            rows = [grown[half, 2 * group + k // 4, k % 4] for k in range(8)]
            for b, row in enumerate(swap_blocks(rows)):
                blocks[8 * half + b, group] = row

    def fill(peer, store):
        for quad in range(groups // 4):
            for v, vec in enumerate(pack_four([blocks[peer, 4 * quad + k] for k in range(4)])):
                store(3 * quad + v, vec)
        store(3 * (groups // 4), jnp.where(lane_ids((8, LANES)) < HALF, blocks[peer, groups - 1], 0.0))

    def block_copy(peer):
        return pltpu.make_async_remote_copy(
            src_ref=packed.at[peer], dst_ref=landed.at[mem], send_sem=block_send.at[peer], recv_sem=block_recv.at[mem],
            device_id={"mem": peer}, device_id_type=MESH,
        )

    @pl.loop(1, tiles)
    def _(j):
        peer = lax.rem(mem + j, tiles)

        def store(v, vec):
            packed[peer, :, pl.ds(LANES * v, LANES)] = vec

        fill(peer, store)
        block_copy(peer).start()

    def keep(v, vec):
        landed[mem, :, pl.ds(LANES * v, LANES)] = vec

    fill(mem, keep)

    @pl.loop(1, tiles)
    def _(j):
        owner = lax.rem(mem + j, tiles)
        pltpu.make_async_remote_copy(
            src_ref=packed.at[owner], dst_ref=landed.at[owner], send_sem=block_send.at[owner],
            recv_sem=block_recv.at[owner], device_id={"mem": owner}, device_id_type=MESH,
        ).wait_recv()

    @pl.loop(0, tiles)
    def _(j):
        out_ref[j] = landed[j]

    @pl.loop(1, tiles)
    def _(j):
        block_copy(lax.rem(mem + j, tiles)).wait_send()

    @pl.when(sp < bands - 1)
    def _():
        down.wait_send()

    @pl.when(sp > 0)
    def _():
        up.wait_send()


def forecast(x, diffusivity, coupling, axis_sizes):
    fields, levels = coupling.shape[0], diffusivity.shape[0]
    layers, members, _ = x.shape
    tiles = axis_sizes[0]
    groups = layers // 2
    width = LANES * (-(-layers * 4 * TILE_COLS // LANES))
    vmem, smem = pl.BlockSpec(memory_space=pltpu.VMEM), pl.BlockSpec(memory_space=pltpu.SMEM)
    return pl.pallas_call(
        functools.partial(forecast_kernel, axis_sizes, fields, levels),
        out_shape=jax.ShapeDtypeStruct((tiles, members, width), F32),
        in_specs=[vmem, smem, smem],
        out_specs=vmem,
        scratch_shapes=[
            pltpu.VMEM((layers, members, 3 * LANES), F32),
            pltpu.VMEM((layers, members, 3 * LANES), F32),
            pltpu.VMEM((2, layers, 4, members, LANES), F32),
            pltpu.VMEM((tiles, groups, members, LANES), F32),
            pltpu.VMEM((tiles, members, width), F32),
            pltpu.VMEM((tiles, members, width), F32),
            pltpu.SemaphoreType.DMA((2,)),
            pltpu.SemaphoreType.DMA((2,)),
            pltpu.SemaphoreType.DMA((tiles,)),
            pltpu.SemaphoreType.DMA((tiles,)),
        ],
        compiler_params=pltpu.CompilerParams(
            collective_id=0, has_side_effects=True, vmem_limit_bytes=32 * 1024 * 1024
        ),
    )(x, diffusivity, coupling)


def return_kernel(axis_sizes, a_ref, out_ref, landed, blocks, send, recv):
    mem = lax.axis_index("mem")
    tiles = axis_sizes[0]
    groups = blocks.shape[1]

    greet(axis_sizes, False)
    await_greetings(axis_sizes, False)

    def block_copy(peer, slot):
        return pltpu.make_async_remote_copy(
            src_ref=a_ref.at[peer], dst_ref=landed.at[slot], send_sem=send.at[peer], recv_sem=recv.at[slot],
            device_id={"mem": peer}, device_id_type=MESH,
        )

    @pl.loop(1, tiles)
    def _(j):
        block_copy(lax.rem(mem + j, tiles), mem).start()

    landed[mem] = a_ref[mem]

    def spread_out(owner):
        for quad in range(groups // 4):
            vecs = [landed[owner, :, pl.ds(LANES * (3 * quad + v), LANES)] for v in range(3)]
            for k, part in enumerate(unpack_four(vecs)):
                blocks[owner, 4 * quad + k] = part
        blocks[owner, groups - 1] = landed[owner, :, pl.ds(LANES * 3 * (groups // 4), LANES)]

    spread_out(mem)

    @pl.loop(1, tiles)
    def _(j):
        owner = lax.rem(mem + tiles - j, tiles)
        block_copy(owner, owner).wait_recv()
        spread_out(owner)

    @pl.loop(0, groups)
    def _(group):
        halves = [swap_blocks([blocks[8 * half + b, group] for b in range(8)]) for half in range(2)]
        for pair in range(4):
            parts = [halves[k % 2][2 * pair + k // 2] for k in range(4)]
            for v, vec in enumerate(pack_four(parts)):
                out_ref[2 * group + pair // 2, :, pl.ds(LANES * (3 * (pair % 2) + v), LANES)] = vec

    @pl.loop(1, tiles)
    def _(j):
        block_copy(lax.rem(mem + j, tiles), mem).wait_send()


def give_back(blocks, layers, axis_sizes):
    tiles, members, width = blocks.shape
    vmem = pl.BlockSpec(memory_space=pltpu.VMEM)
    return pl.pallas_call(
        functools.partial(return_kernel, axis_sizes),
        out_shape=jax.ShapeDtypeStruct((layers, members, 4 * TILE_COLS * tiles), F32),
        in_specs=[vmem],
        out_specs=vmem,
        scratch_shapes=[
            pltpu.VMEM((tiles, members, width), F32),
            pltpu.VMEM((tiles, layers // 2, members, LANES), F32),
            pltpu.SemaphoreType.DMA((tiles,)),
            pltpu.SemaphoreType.DMA((tiles,)),
        ],
        compiler_params=pltpu.CompilerParams(
            collective_id=1, has_side_effects=True, vmem_limit_bytes=32 * 1024 * 1024
        ),
    )(blocks)


def dot(a, b, dims):
    return lax.dot_general(a, b, dims, preferred_element_type=F32)


def split2(x):
    hi = x.astype(BF16)
    lo = (x - hi.astype(F32)).astype(BF16)
    return hi, lo


def split3(x):
    hi = x.astype(BF16)
    rest = x - hi.astype(F32)
    mid = rest.astype(BF16)
    lo = (rest - mid.astype(F32)).astype(BF16)
    return hi, mid, lo


def observation_sums(lists, scales, observed, cells, lanes):
    nobs = observed.shape[1]
    points, nloc = lists.shape
    pieces = jnp.concatenate(split3(scales), axis=0)
    which = lax.broadcasted_iota(jnp.int32, (nobs, nloc), 0)
    row = lax.broadcasted_iota(jnp.int32, (points, nobs), 0)
    per_obs = jnp.zeros((points, nobs), F32)
    for c in range(points):
        picked = jnp.where(lists[c : c + 1, :] == which, 1.0, 0.0).astype(BF16)
        got = dot(pieces, picked, NT)
        got = got[:points] + got[points : 2 * points] + got[2 * points :]
        per_obs = jnp.where(row == c, got, per_obs)
    both = jnp.concatenate(split3(per_obs) + split3(per_obs * observed), axis=0)
    place = lax.broadcasted_iota(jnp.int32, (lanes, nobs), 0)
    spots = jnp.where(cells == place, 1.0, 0.0).astype(BF16)
    got = dot(both, spots, NT)
    p = points
    weight = got[:p] + got[p : 2 * p] + got[2 * p : 3 * p]
    total = got[3 * p : 4 * p] + got[4 * p : 5 * p] + got[5 * p :]
    return weight, total


def factor_inverses(r_ref, members):
    p = COARSE
    lane = lax.broadcasted_iota(jnp.int32, (p, members), 1)

    def spread(v, i):
        return jnp.broadcast_to(v[:, i : i + 1], v.shape)

    for k0 in range(0, members, PIVOTS):
        rows = [r_ref[pl.ds(p * (k0 + t), p), :] for t in range(PIVOTS)]
        done = []
        for t in range(PIVOTS):
            k = k0 + t
            pivot = spread(rows[t], k)
            own = jnp.where(lane == k, 1.0, rows[t])
            unit = own * (1.0 / pivot)
            for s in range(t + 1, PIVOTS):
                rows[s] = jnp.where(lane == k, 0.0, rows[s]) - spread(rows[t], k0 + s) * unit
            done.append(own * lax.rsqrt(pivot))
        for t in range(PIVOTS):
            r_ref[pl.ds(p * (k0 + t), p), :] = jnp.where(lane <= k0 + t, done[t], 0.0)
        block = (lane >= k0) & (lane < k0 + PIVOTS)
        kept = [jnp.where(block & (lane > k0 + t), 0.0, done[t]) for t in range(PIVOTS)]
        for i in range(k0 + PIVOTS, members):
            acc = jnp.where(block, 0.0, r_ref[pl.ds(p * i, p), :])
            for t in range(PIVOTS):
                acc = acc - spread(done[t], i) * kept[t]
            r_ref[pl.ds(p * i, p), :] = acc


def analysis_kernel(field_ref, lists_ref, scales_ref, observed_ref, cells_ref, hats_ref, out_ref, r_ref):
    members, lanes = field_ref.shape
    p = COARSE
    weight, total = observation_sums(lists_ref[...], scales_ref[...], observed_ref[...], cells_ref[...], lanes)
    field = field_ref[...]
    mean = jnp.sum(field, axis=0, keepdims=True) * (1.0 / members)
    dev = field - mean
    hi, lo = split2(dev)
    lead = float(members - 1)
    eye = jnp.where(
        lax.broadcasted_iota(jnp.int32, (members, members), 0) == lax.broadcasted_iota(jnp.int32, (members, members), 1),
        lead,
        0.0,
    )
    for c in range(p):
        s_hi, s_lo = split2(dev * weight[c : c + 1, :])
        g = dot(s_hi, hi, NT) + dot(s_hi, lo, NT) + dot(s_lo, hi, NT) + eye
        r_ref[pl.ds(c, members, stride=p), :] = g
    gap = total - mean * weight
    g_hi, g_lo = split2(gap)
    pull = dot(g_hi, hi, NT) + dot(g_hi, lo, NT) + dot(g_lo, hi, NT)

    factor_inverses(r_ref, members)

    root = lead**0.5
    moved = jnp.zeros((members, lanes), F32)
    for c in range(p):
        m = r_ref[pl.ds(c, members, stride=p), :]
        y = lax.dot_general(pull[c : c + 1, :], m, NT, precision=lax.Precision.HIGHEST, preferred_element_type=F32)
        w = lax.dot_general(y, m, NN, precision=lax.Precision.HIGHEST, preferred_element_type=F32)
        w_hi, w_lo = split2(m * root + w)
        moved = moved + hats_ref[c : c + 1, :] * (dot(w_hi, hi, NN) + dot(w_hi, lo, NN) + dot(w_lo, hi, NN))
    out_ref[...] = mean + moved


def analyse(field, lists, scales, observed, cells, hats):
    members, lanes = field.shape
    return pl.pallas_call(
        analysis_kernel,
        out_shape=jax.ShapeDtypeStruct((members, lanes), F32),
        in_specs=[pl.BlockSpec(memory_space=pltpu.VMEM)] * 6,
        out_specs=pl.BlockSpec(memory_space=pltpu.VMEM),
        scratch_shapes=[pltpu.VMEM((COARSE * members, members), F32)],
        compiler_params=pltpu.CompilerParams(vmem_limit_bytes=48 * 1024 * 1024),
    )(field, lists, scales, observed, cells, hats)


def hat_table(row_stack, cols):
    row_pos = jnp.arange(row_stack, dtype=jnp.float32)
    col_pos = jnp.arange(cols, dtype=jnp.float32)
    span_y = (row_stack - 1) / (GY - 1)
    span_x = (cols - 1) / (GX - 1)
    centre_y = jnp.arange(GY, dtype=jnp.float32) * span_y
    centre_x = jnp.arange(GX, dtype=jnp.float32) * span_x
    hat_y = jnp.maximum(0.0, 1.0 - jnp.abs(row_pos[None, :] - centre_y[:, None]) / span_y)
    hat_x = jnp.maximum(0.0, 1.0 - jnp.abs(col_pos[None, :] - centre_x[:, None]) / span_x)
    hats = hat_y[:, None, :, None] * hat_x[None, :, None, :]
    return hats.reshape(GY * GX, row_stack * cols)


def on_device(
    axis_sizes,
    cycle_start_state,
    diffusivity,
    coupling,
    observation_value,
    observation_cell,
    observation_lists,
    localization_weight,
):
    members, fields, levels, span = cycle_start_state.shape
    layers = fields * levels
    x = cycle_start_state.transpose(1, 2, 0, 3).reshape(layers, members, span)
    columns = forecast(x, diffusivity, coupling, axis_sizes)
    tiles, _, width = columns.shape
    hats = jnp.tile(hat_table(4, TILE_COLS), (1, layers))
    analysed = analyse(
        columns.reshape(tiles * members, width),
        observation_lists[0, 0],
        localization_weight[0, 0],
        observation_value[0],
        observation_cell[0],
        jnp.pad(hats, ((0, 0), (0, width - hats.shape[1]))),
    )
    y = give_back(analysed.reshape(tiles, members, width), layers, axis_sizes)
    return y.reshape(fields, levels, members, span).transpose(2, 0, 1, 3)


def solution(mesh):
    in_specs = (
        P("mem", None, None, "sp"),
        P(),
        P(),
        P("sp", "mem", None),
        P("sp", "mem", None),
        P("sp", "mem", None, None),
        P("sp", "mem", None, None),
    )
    out_specs = P("mem", None, None, "sp")
    axis_sizes = (mesh.shape["mem"], mesh.shape["sp"])
    return jax.shard_map(
        functools.partial(on_device, axis_sizes), mesh=mesh, in_specs=in_specs, out_specs=out_specs, check_vma=False
    )
```

```python
import functools

import jax
import jax.numpy as jnp
from jax import lax
from jax.experimental import pallas as pl
from jax.experimental.pallas import tpu as pltpu
from jax.sharding import PartitionSpec as P

GX = 4
GY = 2
COARSE = 8
PIVOTS = 8
PANEL = 16
F32 = jnp.float32
BF16 = jnp.bfloat16
NT = (((1,), (1,)), ((), ()))
NN = (((1,), (0,)), ((), ()))
TN = (((0,), (0,)), ((), ()))
MESH = pl.DeviceIdType.MESH
LANES = 128
TILE_ROWS = 4
TILE_COLS = 12
HALF = 96


def dot(a, b, dims):
    return lax.dot_general(a, b, dims, preferred_element_type=F32)


def split2(x):
    hi = x.astype(BF16)
    lo = (x - hi.astype(F32)).astype(BF16)
    return hi, lo


def split3(x):
    hi = x.astype(BF16)
    rest = x - hi.astype(F32)
    mid = rest.astype(BF16)
    lo = (rest - mid.astype(F32)).astype(BF16)
    return hi, mid, lo


def observation_sums(lists, scales, observed, cells, lanes):
    nobs = observed.shape[1]
    points, nloc = lists.shape
    pieces = jnp.concatenate(split3(scales), axis=0)
    which = lax.broadcasted_iota(jnp.int32, (nobs, nloc), 0)
    row = lax.broadcasted_iota(jnp.int32, (points, nobs), 0)
    per_obs = jnp.zeros((points, nobs), F32)
    for c in range(points):
        picked = jnp.where(lists[c : c + 1, :] == which, 1.0, 0.0).astype(BF16)
        got = dot(pieces, picked, NT)
        got = got[:points] + got[points : 2 * points] + got[2 * points :]
        per_obs = jnp.where(row == c, got, per_obs)
    both = jnp.concatenate(split3(per_obs) + split3(per_obs * observed), axis=0)
    place = lax.broadcasted_iota(jnp.int32, (lanes, nobs), 0)
    spots = jnp.where(cells == place, 1.0, 0.0).astype(BF16)
    got = dot(both, spots, NT)
    p = points
    weight = got[:p] + got[p : 2 * p] + got[2 * p : 3 * p]
    total = got[3 * p : 4 * p] + got[4 * p : 5 * p] + got[5 * p :]
    return weight, total


def factor_inverses(g_ref, r_ref):
    p, members, _ = g_ref.shape
    lane = lax.broadcasted_iota(jnp.int32, (p, members), 1)
    panel_lane = lax.broadcasted_iota(jnp.int32, (PANEL, members), 1)
    panel_row = lax.broadcasted_iota(jnp.int32, (PANEL, members), 0)

    def spread(v, i):
        return jnp.broadcast_to(v[:, i : i + 1], v.shape)

    for b0 in range(0, members, PANEL):
        for c in range(p):
            r_ref[pl.ds(c, PANEL, stride=p), :] = g_ref[c, pl.ds(b0, PANEL), :]
        for k0 in range(0, PANEL, PIVOTS):
            at = b0 + k0
            rows = [r_ref[pl.ds(p * (k0 + t), p), :] for t in range(PIVOTS)]
            e = [[spread(rows[t], at + s) for t in range(s + 1)] for s in range(PIVOTS)]
            block = (lane >= at) & (lane < at + PIVOTS)
            rows = [jnp.where(block, jnp.where(lane == at + t, 1.0, 0.0), rows[t]) for t in range(PIVOTS)]
            for t in range(PIVOTS):
                inverse = 1.0 / e[t][t]
                for s in range(t + 1, PIVOTS):
                    ratio = e[s][t] * inverse
                    for j in range(t + 1, s + 1):
                        e[s][j] = e[s][j] - ratio * e[j][t]
                    rows[s] = rows[s] - ratio * rows[t]
            done = [rows[t] * lax.rsqrt(e[t][t]) for t in range(PIVOTS)]
            for t in range(PIVOTS):
                r_ref[pl.ds(p * (k0 + t), p), :] = done[t]
            for i in range(k0 + PIVOTS, PANEL):
                acc = jnp.where(block, 0.0, r_ref[pl.ds(p * i, p), :])
                for t in range(PIVOTS):
                    acc = acc - spread(done[t], b0 + i) * done[t]
                r_ref[pl.ds(p * i, p), :] = acc
        end = b0 + PANEL
        for c in range(p):
            v = r_ref[pl.ds(c, PANEL, stride=p), :]
            lower = panel_lane <= panel_row + b0
            g_ref[c, pl.ds(b0, PANEL), :] = jnp.where(lower, v, 0.0)
            if end < members:
                hi, mid, lo = split3(v)
                kept = jnp.where(lower | (panel_lane >= end), 1.0, 0.0).astype(BF16)
                k_hi, k_mid, k_lo = hi * kept, mid * kept, lo * kept
                left = jnp.concatenate([hi, hi, mid, hi, mid, lo], axis=0)
                right = jnp.concatenate([k_hi, k_mid, k_hi, k_lo, k_mid, k_hi], axis=0)
                change = dot(left[:, end:] if end % 128 == 0 else left, right, TN)
                below = g_ref[c, pl.ds(end, members - end), :]
                low_lane = lax.broadcasted_iota(jnp.int32, below.shape, 1)
                below = jnp.where((low_lane >= b0) & (low_lane < end), 0.0, below)
                g_ref[c, pl.ds(end, members - end), :] = below - change[end:, :]


def lane_ids(shape):
    return lax.broadcasted_iota(jnp.int32, shape, len(shape) - 1)


def turn(x, shift):
    return pltpu.roll(x, shift % LANES, x.ndim - 1)


def swap_blocks(rows):
    rows = list(rows)
    lane = lane_ids(rows[0].shape)
    for step in (4, 2, 1):
        width = TILE_COLS * step
        keep = lane % (2 * width) < width
        for a in range(8):
            if a & step:
                continue
            low, high = rows[a], rows[a + step]
            rows[a] = jnp.where(keep, low, turn(high, width))
            rows[a + step] = jnp.where(keep, turn(low, -width), high)
    return rows


def pack_four(parts):
    lane = lane_ids(parts[0].shape)
    one, two, three = turn(parts[1], 96), turn(parts[2], 64), turn(parts[3], 32)
    return [
        jnp.where(lane < 96, parts[0], one),
        jnp.where(lane < 64, one, two),
        jnp.where(lane < 32, two, three),
    ]


def unpack_four(vecs):
    lane = lane_ids(vecs[0].shape)
    return [
        vecs[0],
        turn(jnp.where(lane < 64, vecs[1], vecs[0]), -96),
        turn(jnp.where(lane < 64, vecs[2], vecs[1]), -64),
        turn(vecs[2], -32),
    ]


def row_halves(vecs):
    lane = lane_ids(vecs[0].shape)
    first, middle, last = vecs
    return [
        (first, jnp.where(lane < 64, middle, first)),
        (turn(jnp.where(lane < 64, last, middle), 64), turn(last, 64)),
    ]


def time_step(rows, diffusion, mix):
    fields, count = len(rows), len(rows[0])
    lane = lane_ids(rows[0][0][0].shape)
    out = [[None] * (count - 2) for _ in range(fields)]
    for r in range(1, count - 1):
        pair = [[None, None] for _ in range(fields)]
        for h in range(2):
            for f in range(fields):
                center = rows[f][r][h]
                before, after = turn(center, 1), turn(center, -1)
                if h == 0:
                    before = jnp.where(lane == 0, 0.0, before)
                else:
                    after = jnp.where(lane == 63, 0.0, after)
                around = (rows[f][r - 1][h] + rows[f][r + 1][h]) + (before + after)
                new = diffusion * around
                for g in range(fields):
                    new = new + mix[f][g] * rows[g][r][h]
                pair[f][h] = new
        for f in range(fields):
            out[f][r - 1] = tuple(pair[f])
    return out


def hat_rows(lanes):
    lane = lax.broadcasted_iota(jnp.int32, (1, lanes), 1) % (TILE_ROWS * TILE_COLS)
    row, col = (lane // TILE_COLS).astype(F32), (lane % TILE_COLS).astype(F32)
    span_y, span_x = (TILE_ROWS - 1) / (GY - 1), (TILE_COLS - 1) / (GX - 1)
    hat_y = [jnp.maximum(0.0, 1.0 - jnp.abs(row - i * span_y) / span_y) for i in range(GY)]
    hat_x = [jnp.maximum(0.0, 1.0 - jnp.abs(col - j * span_x) / span_x) for j in range(GX)]
    return [y * x for y in hat_y for x in hat_x]


def analyse(field, weight, total, g_ref, r_ref):
    members, lanes = field.shape
    p = COARSE
    mean = jnp.sum(field, axis=0, keepdims=True) * (1.0 / members)
    dev = field - mean
    hi, mid, lo = split3(dev)
    both = jnp.concatenate([hi, mid], axis=0)
    lead = float(members - 1)
    eye = jnp.where(
        lax.broadcasted_iota(jnp.int32, (members, members), 0) == lax.broadcasted_iota(jnp.int32, (members, members), 1),
        lead,
        0.0,
    )
    for c in range(p):
        s_hi, s_mid, s_lo = split3(dev * weight[c : c + 1, :])
        g = dot(s_hi, both, NT) + dot(s_mid, both, NT)
        g_ref[c] = g[:, :members] + g[:, members:] + (dot(s_hi, lo, NT) + dot(s_lo, hi, NT)) + eye
    gap = total - mean * weight
    g_hi, g_mid, g_lo = split3(gap)
    pull = dot(g_hi, both, NT) + dot(g_mid, both, NT)
    pull = pull[:, :members] + pull[:, members:] + (dot(g_hi, lo, NT) + dot(g_lo, hi, NT))

    factor_inverses(g_ref, r_ref)

    root = lead**0.5
    ms = [g_ref[c] for c in range(p)]
    high = dict(precision=lax.Precision.HIGHEST, preferred_element_type=F32)
    ys = [lax.dot_general(pull[c : c + 1, :], ms[c], NT, **high) for c in range(p)]
    ws = [lax.dot_general(ys[c], ms[c], NN, **high) for c in range(p)]
    hats = hat_rows(lanes)
    moved = mean
    for c in range(p):
        w_hi, w_lo = split2(ms[c] * root + ws[c])
        twice = jnp.concatenate([w_hi, w_hi], axis=1)
        moved = moved + hats[c] * (dot(twice, both, NN) + dot(w_lo, hi, NN))
    return moved


def peer_order(mem):
    side, place, core = mem // 8, mem // 2 % 4, mem % 2
    far_first = [(1, 2), (0, 2), (1, 1), (1, 3), (1, 0), (0, 1), (0, 3), (0, 0)]
    peers = []
    for d_side, d_place in far_first:
        for d_core in range(2):
            if d_side or d_place or d_core:
                peers.append((side + d_side) % 2 * 8 + (place + d_place) % 4 * 2 + (core + d_core) % 2)
    return peers


def cycle_kernel(
    axis_sizes, fields, levels, x_ref, diffusion_ref, coupling_ref, observed_ref, cells_ref, lists_ref, scales_ref, out_ref,
    xs, north, south, grown, blocks, packed, landed, result, returned, weight_ref, total_ref, g_ref, r_ref,
    load_sem, halo_send, halo_recv, block_send, block_recv, back_send, back_recv,
):
    mem, sp = lax.axis_index("mem"), lax.axis_index("sp")
    tiles, bands = axis_sizes
    layers = fields * levels
    groups = layers // 2
    two = 3 * LANES
    members, width = packed.shape[1:]
    peers = peer_order(mem)

    load = pltpu.make_async_copy(x_ref, xs, load_sem)
    load.start()
    barrier = pltpu.get_barrier_semaphore()

    @pl.when(sp > 0)
    def _():
        pl.semaphore_signal(barrier, inc=1, device_id={"sp": sp - 1}, device_id_type=MESH)

    @pl.when(sp < bands - 1)
    def _():
        pl.semaphore_signal(barrier, inc=1, device_id={"sp": sp + 1}, device_id_type=MESH)

    for peer in peers:
        pl.semaphore_signal(barrier, inc=1, device_id={"mem": peer}, device_id_type=MESH)
    pl.semaphore_wait(barrier, tiles - 1 + jnp.minimum(sp, 1) + jnp.minimum(bands - 1 - sp, 1))

    down = pltpu.make_async_remote_copy(
        src_ref=x_ref.at[:, :, pl.ds(two, two)], dst_ref=north, send_sem=halo_send.at[0], recv_sem=halo_recv.at[0],
        device_id={"sp": lax.rem(sp + 1, bands)}, device_id_type=MESH,
    )
    up = pltpu.make_async_remote_copy(
        src_ref=x_ref.at[:, :, pl.ds(0, two)], dst_ref=south, send_sem=halo_send.at[1], recv_sem=halo_recv.at[1],
        device_id={"sp": lax.rem(sp + bands - 1, bands)}, device_id_type=MESH,
    )

    @pl.when(sp < bands - 1)
    def _():
        down.start()

    @pl.when(sp > 0)
    def _():
        up.start()

    @pl.when(sp == 0)
    def _():
        north[...] = jnp.zeros_like(north)

    @pl.when(sp == bands - 1)
    def _():
        south[...] = jnp.zeros_like(south)

    weight, total = observation_sums(lists_ref[...], scales_ref[...], observed_ref[...], cells_ref[...], width)
    weight_ref[...] = weight
    total_ref[...] = total
    load.wait()

    @pl.when(sp > 0)
    def _():
        down.wait_recv()

    @pl.when(sp < bands - 1)
    def _():
        up.wait_recv()

    inside_north = jnp.minimum(sp, 1).astype(F32)
    inside_south = jnp.minimum(bands - 1 - sp, 1).astype(F32)

    @pl.loop(0, levels)
    def _(level):
        diffusion = diffusion_ref[level]
        own = 1.0 - 4.0 * diffusion
        mix = [[coupling_ref[f, g] + own if f == g else coupling_ref[f, g] for g in range(fields)] for f in range(fields)]
        rows = []
        for f in range(fields):
            layer = f * levels + level
            line = []
            for ref, starts in ((north, (0,)), (xs, (0, two)), (south, (0,))):
                for start in starts:
                    line += row_halves([ref[layer, :, pl.ds(start + LANES * v, LANES)] for v in range(3)])
            rows.append(line)
        middle = time_step(rows, diffusion, mix)
        for f in range(fields):
            middle[f][0] = tuple(inside_north * v for v in middle[f][0])
            middle[f][-1] = tuple(inside_south * v for v in middle[f][-1])
        final = time_step(middle, diffusion, mix)
        for f in range(fields):
            layer = f * levels + level
            for r in range(len(final[f])):
                grown[0, layer, r] = final[f][r][0]
                grown[1, layer, r] = turn(final[f][r][1], 32)

    for half in range(2):

        @pl.loop(0, groups)
        def _(group):
            rows = [grown[half, 2 * group + k // 4, k % 4] for k in range(8)]
            for b, row in enumerate(swap_blocks(rows)):
                blocks[8 * half + b, group] = row

    def fill(peer, store):
        for quad in range(groups // 4):
            for v, vec in enumerate(pack_four([blocks[peer, 4 * quad + k] for k in range(4)])):
                store(3 * quad + v, vec)
        store(3 * (groups // 4), jnp.where(lane_ids((members, LANES)) < HALF, blocks[peer, groups - 1], 0.0))

    def block_copy(peer, slot):
        return pltpu.make_async_remote_copy(
            src_ref=packed.at[peer], dst_ref=landed.at[slot], send_sem=block_send.at[peer], recv_sem=block_recv.at[slot],
            device_id={"mem": peer}, device_id_type=MESH,
        )

    for peer in peers:

        def store(v, vec):
            packed[peer, :, pl.ds(LANES * v, LANES)] = vec

        fill(peer, store)
        block_copy(peer, mem).start()

    def keep(v, vec):
        landed[mem, :, pl.ds(LANES * v, LANES)] = vec

    fill(mem, keep)
    for peer in peers[::-1]:
        block_copy(peer, peer).wait_recv()

    moved = analyse(landed[...].reshape(tiles * members, width), weight_ref[...], total_ref[...], g_ref, r_ref)
    result[...] = moved.reshape(tiles, members, width)

    def back_copy(peer, slot):
        return pltpu.make_async_remote_copy(
            src_ref=result.at[peer], dst_ref=returned.at[slot], send_sem=back_send.at[peer], recv_sem=back_recv.at[slot],
            device_id={"mem": peer}, device_id_type=MESH,
        )

    for peer in peers:
        back_copy(peer, mem).start()
    for peer in peers:
        block_copy(peer, mem).wait_send()

    @pl.when(sp < bands - 1)
    def _():
        down.wait_send()

    @pl.when(sp > 0)
    def _():
        up.wait_send()

    def spread_out(ref, owner):
        for quad in range(groups // 4):
            vecs = [ref[owner, :, pl.ds(LANES * (3 * quad + v), LANES)] for v in range(3)]
            for k, part in enumerate(unpack_four(vecs)):
                blocks[owner, 4 * quad + k] = part
        blocks[owner, groups - 1] = ref[owner, :, pl.ds(LANES * 3 * (groups // 4), LANES)]

    spread_out(result, mem)
    for peer in peers[::-1]:
        back_copy(peer, peer).wait_recv()
        spread_out(returned, peer)

    @pl.loop(0, groups)
    def _(group):
        halves = [swap_blocks([blocks[8 * half + b, group] for b in range(8)]) for half in range(2)]
        for pair in range(4):
            parts = [halves[k % 2][2 * pair + k // 2] for k in range(4)]
            for v, vec in enumerate(pack_four(parts)):
                out_ref[2 * group + pair // 2, :, pl.ds(LANES * (3 * (pair % 2) + v), LANES)] = vec

    for peer in peers:
        back_copy(peer, mem).wait_send()


def cycle(x, diffusivity, coupling, observed, cells, lists, scales, axis_sizes):
    fields, levels = coupling.shape[0], diffusivity.shape[0]
    layers, members, span = x.shape
    tiles = axis_sizes[0]
    everyone = tiles * members
    width = LANES * (-(-layers * TILE_ROWS * TILE_COLS // LANES))
    vmem, smem = pl.BlockSpec(memory_space=pltpu.VMEM), pl.BlockSpec(memory_space=pltpu.SMEM)
    block = pltpu.VMEM((tiles, members, width), F32)
    halo = pltpu.VMEM((layers, members, 3 * LANES), F32)
    semaphores = pltpu.SemaphoreType.DMA((tiles,))
    return pl.pallas_call(
        functools.partial(cycle_kernel, axis_sizes, fields, levels),
        out_shape=jax.ShapeDtypeStruct((layers, members, span), F32),
        in_specs=[pl.BlockSpec(memory_space=pl.ANY), smem, smem, vmem, vmem, vmem, vmem],
        out_specs=vmem,
        scratch_shapes=[
            pltpu.VMEM((layers, members, span), F32),
            halo,
            halo,
            pltpu.VMEM((2, layers, TILE_ROWS, members, LANES), F32),
            pltpu.VMEM((tiles, layers // 2, members, LANES), F32),
            block,
            block,
            block,
            block,
            pltpu.VMEM((COARSE, width), F32),
            pltpu.VMEM((COARSE, width), F32),
            pltpu.VMEM((COARSE, everyone, everyone), F32),
            pltpu.VMEM((COARSE * PANEL, everyone), F32),
            pltpu.SemaphoreType.DMA,
            pltpu.SemaphoreType.DMA((2,)),
            pltpu.SemaphoreType.DMA((2,)),
            semaphores,
            semaphores,
            semaphores,
            semaphores,
        ],
        compiler_params=pltpu.CompilerParams(
            collective_id=0, has_side_effects=True, vmem_limit_bytes=56 * 1024 * 1024
        ),
    )(x, diffusivity, coupling, observed, cells, lists, scales)


def on_device(
    axis_sizes,
    cycle_start_state,
    diffusivity,
    coupling,
    observation_value,
    observation_cell,
    observation_lists,
    localization_weight,
):
    members, fields, levels, span = cycle_start_state.shape
    layers = fields * levels
    y = cycle(
        cycle_start_state.transpose(1, 2, 0, 3).reshape(layers, members, span),
        diffusivity,
        coupling,
        observation_value[0],
        observation_cell[0],
        observation_lists[0, 0],
        localization_weight[0, 0],
        axis_sizes,
    )
    return y.reshape(fields, levels, members, span).transpose(2, 0, 1, 3)


def solution(mesh):
    in_specs = (
        P("mem", None, None, "sp"),
        P(),
        P(),
        P("sp", "mem", None),
        P("sp", "mem", None),
        P("sp", "mem", None, None),
        P("sp", "mem", None, None),
    )
    out_specs = P("mem", None, None, "sp")
    axis_sizes = (mesh.shape["mem"], mesh.shape["sp"])
    return jax.shard_map(
        functools.partial(on_device, axis_sizes), mesh=mesh, in_specs=in_specs, out_specs=out_specs, check_vma=False
    )
```

```python
import functools

import jax
import jax.numpy as jnp
from jax import lax
from jax.experimental import pallas as pl
from jax.experimental.pallas import tpu as pltpu
from jax.sharding import PartitionSpec as P

GX = 4
GY = 2
COARSE = 8
PIVOTS = 8
PANEL = 16
F32 = jnp.float32
BF16 = jnp.bfloat16
NT = (((1,), (1,)), ((), ()))
NN = (((1,), (0,)), ((), ()))
TN = (((0,), (0,)), ((), ()))
MESH = pl.DeviceIdType.MESH
LANES = 128
TILE_ROWS = 4
TILE_COLS = 12
HALF = 96


def dot(a, b, dims):
    return lax.dot_general(a, b, dims, preferred_element_type=F32)


def split2(x):
    hi = x.astype(BF16)
    lo = (x - hi.astype(F32)).astype(BF16)
    return hi, lo


def split3(x):
    hi = x.astype(BF16)
    rest = x - hi.astype(F32)
    mid = rest.astype(BF16)
    lo = (rest - mid.astype(F32)).astype(BF16)
    return hi, mid, lo


def observation_sums(lists, scales, observed, cells, lanes):
    nobs = observed.shape[1]
    points, nloc = lists.shape
    pieces = jnp.concatenate(split3(scales), axis=0)
    which = lax.broadcasted_iota(jnp.int32, (nobs, nloc), 0)
    row = lax.broadcasted_iota(jnp.int32, (points, nobs), 0)
    per_obs = jnp.zeros((points, nobs), F32)
    for c in range(points):
        picked = jnp.where(lists[c : c + 1, :] == which, 1.0, 0.0).astype(BF16)
        got = dot(pieces, picked, NT)
        got = got[:points] + got[points : 2 * points] + got[2 * points :]
        per_obs = jnp.where(row == c, got, per_obs)
    both = jnp.concatenate(split3(per_obs) + split3(per_obs * observed), axis=0)
    place = lax.broadcasted_iota(jnp.int32, (lanes, nobs), 0)
    spots = jnp.where(cells == place, 1.0, 0.0).astype(BF16)
    got = dot(both, spots, NT)
    p = points
    weight = got[:p] + got[p : 2 * p] + got[2 * p : 3 * p]
    total = got[3 * p : 4 * p] + got[4 * p : 5 * p] + got[5 * p :]
    return weight, total


def factor_inverses(g_ref, r_ref):
    p, members, _ = g_ref.shape
    lane = lax.broadcasted_iota(jnp.int32, (p, members), 1)
    panel_lane = lax.broadcasted_iota(jnp.int32, (PANEL, members), 1)
    panel_row = lax.broadcasted_iota(jnp.int32, (PANEL, members), 0)

    def spread(v, i):
        return jnp.broadcast_to(v[:, i : i + 1], v.shape)

    for b0 in range(0, members, PANEL):
        for c in range(p):
            r_ref[pl.ds(c, PANEL, stride=p), :] = g_ref[c, pl.ds(b0, PANEL), :]
        for k0 in range(0, PANEL, PIVOTS):
            at = b0 + k0
            rows = [r_ref[pl.ds(p * (k0 + t), p), :] for t in range(PIVOTS)]
            e = [[spread(rows[t], at + s) for t in range(s + 1)] for s in range(PIVOTS)]
            block = (lane >= at) & (lane < at + PIVOTS)
            rows = [jnp.where(block, jnp.where(lane == at + t, 1.0, 0.0), rows[t]) for t in range(PIVOTS)]
            for t in range(PIVOTS):
                inverse = 1.0 / e[t][t]
                for s in range(t + 1, PIVOTS):
                    ratio = e[s][t] * inverse
                    for j in range(t + 1, s + 1):
                        e[s][j] = e[s][j] - ratio * e[j][t]
                    rows[s] = rows[s] - ratio * rows[t]
            done = [rows[t] * lax.rsqrt(e[t][t]) for t in range(PIVOTS)]
            for t in range(PIVOTS):
                r_ref[pl.ds(p * (k0 + t), p), :] = done[t]
            for i in range(k0 + PIVOTS, PANEL):
                acc = jnp.where(block, 0.0, r_ref[pl.ds(p * i, p), :])
                for t in range(PIVOTS):
                    acc = acc - spread(done[t], b0 + i) * done[t]
                r_ref[pl.ds(p * i, p), :] = acc
        end = b0 + PANEL
        for c in range(p):
            v = r_ref[pl.ds(c, PANEL, stride=p), :]
            lower = panel_lane <= panel_row + b0
            g_ref[c, pl.ds(b0, PANEL), :] = jnp.where(lower, v, 0.0)
            if end < members:
                hi, mid, lo = split3(v)
                kept = jnp.where(lower | (panel_lane >= end), 1.0, 0.0).astype(BF16)
                k_hi, k_mid, k_lo = hi * kept, mid * kept, lo * kept
                left = jnp.concatenate([hi, hi, mid, hi, mid, lo], axis=0)
                right = jnp.concatenate([k_hi, k_mid, k_hi, k_lo, k_mid, k_hi], axis=0)
                change = dot(left[:, end:] if end % 128 == 0 else left, right, TN)
                below = g_ref[c, pl.ds(end, members - end), :]
                low_lane = lax.broadcasted_iota(jnp.int32, below.shape, 1)
                below = jnp.where((low_lane >= b0) & (low_lane < end), 0.0, below)
                g_ref[c, pl.ds(end, members - end), :] = below - change[end:, :]


def lane_ids(shape):
    return lax.broadcasted_iota(jnp.int32, shape, len(shape) - 1)


def turn(x, shift):
    return pltpu.roll(x, shift % LANES, x.ndim - 1)


def swap_blocks(rows):
    rows = list(rows)
    lane = lane_ids(rows[0].shape)
    edge = [TILE_COLS * k for k in range(9)]
    between = [(lane >= edge[k]) & (lane < edge[k + 1]) for k in range(8)]
    keeps = {
        4: lane < edge[4],
        2: (lane < edge[2]) | ((lane >= edge[4]) & (lane < edge[6])),
        1: (between[0] | between[2]) | (between[4] | between[6]),
    }
    for step in (4, 2, 1):
        width = TILE_COLS * step
        keep = keeps[step]
        for a in range(8):
            if a & step:
                continue
            low, high = rows[a], rows[a + step]
            rows[a] = jnp.where(keep, low, turn(high, width))
            rows[a + step] = jnp.where(keep, turn(low, -width), high)
    return rows


def pack_four(parts):
    lane = lane_ids(parts[0].shape)
    one, two, three = turn(parts[1], 96), turn(parts[2], 64), turn(parts[3], 32)
    return [
        jnp.where(lane < 96, parts[0], one),
        jnp.where(lane < 64, one, two),
        jnp.where(lane < 32, two, three),
    ]


def unpack_four(vecs):
    lane = lane_ids(vecs[0].shape)
    return [
        vecs[0],
        turn(jnp.where(lane < 64, vecs[1], vecs[0]), -96),
        turn(jnp.where(lane < 64, vecs[2], vecs[1]), -64),
        turn(vecs[2], -32),
    ]


def row_halves(vecs):
    lane = lane_ids(vecs[0].shape)
    first, middle, last = vecs
    return [
        (first, jnp.where(lane < 64, middle, first)),
        (turn(jnp.where(lane < 64, last, middle), 64), turn(last, 64)),
    ]


def time_step(rows, diffusion, mix):
    fields, count = len(rows), len(rows[0])
    lane = lane_ids(rows[0][0][0].shape)
    out = [[None] * (count - 2) for _ in range(fields)]
    for r in range(1, count - 1):
        pair = [[None, None] for _ in range(fields)]
        for h in range(2):
            for f in range(fields):
                center = rows[f][r][h]
                before, after = turn(center, 1), turn(center, -1)
                if h == 0:
                    before = jnp.where(lane == 0, 0.0, before)
                else:
                    after = jnp.where(lane == 63, 0.0, after)
                around = (rows[f][r - 1][h] + rows[f][r + 1][h]) + (before + after)
                new = diffusion * around
                for g in range(fields):
                    new = new + mix[f][g] * rows[g][r][h]
                pair[f][h] = new
        for f in range(fields):
            out[f][r - 1] = tuple(pair[f])
    return out


def hat_rows(lanes):
    lane = lax.broadcasted_iota(jnp.int32, (1, lanes), 1) % (TILE_ROWS * TILE_COLS)
    row, col = (lane // TILE_COLS).astype(F32), (lane % TILE_COLS).astype(F32)
    span_y, span_x = (TILE_ROWS - 1) / (GY - 1), (TILE_COLS - 1) / (GX - 1)
    hat_y = [jnp.maximum(0.0, 1.0 - jnp.abs(row - i * span_y) / span_y) for i in range(GY)]
    hat_x = [jnp.maximum(0.0, 1.0 - jnp.abs(col - j * span_x) / span_x) for j in range(GX)]
    return [y * x for y in hat_y for x in hat_x]


def analyse(field, weight, total, g_ref, r_ref):
    members, lanes = field.shape
    p = COARSE
    mean = jnp.sum(field, axis=0, keepdims=True) * (1.0 / members)
    dev = field - mean
    hi, mid, lo = split3(dev)
    both = jnp.concatenate([hi, mid], axis=0)
    lead = float(members - 1)
    eye = jnp.where(
        lax.broadcasted_iota(jnp.int32, (members, members), 0) == lax.broadcasted_iota(jnp.int32, (members, members), 1),
        lead,
        0.0,
    )
    for c in range(p):
        s_hi, s_mid, s_lo = split3(dev * weight[c : c + 1, :])
        g = dot(s_hi, both, NT) + dot(s_mid, both, NT)
        g_ref[c] = g[:, :members] + g[:, members:] + (dot(s_hi, lo, NT) + dot(s_lo, hi, NT)) + eye
    gap = total - mean * weight
    g_hi, g_mid, g_lo = split3(gap)
    pull = dot(g_hi, both, NT) + dot(g_mid, both, NT)
    pull = pull[:, :members] + pull[:, members:] + (dot(g_hi, lo, NT) + dot(g_lo, hi, NT))

    factor_inverses(g_ref, r_ref)

    root = lead**0.5
    ms = [g_ref[c] for c in range(p)]
    high = dict(precision=lax.Precision.HIGHEST, preferred_element_type=F32)
    ys = [lax.dot_general(pull[c : c + 1, :], ms[c], NT, **high) for c in range(p)]
    ws = [lax.dot_general(ys[c], ms[c], NN, **high) for c in range(p)]
    hats = hat_rows(lanes)
    moved = mean
    for c in range(p):
        w_hi, w_lo = split2(ms[c] * root + ws[c])
        twice = jnp.concatenate([w_hi, w_hi], axis=1)
        moved = moved + hats[c] * (dot(twice, both, NN) + dot(w_lo, hi, NN))
    return moved


def peer_order(mem):
    side, place, core = mem // 8, mem // 2 % 4, mem % 2
    far_first = [(1, 2), (0, 2), (1, 1), (1, 3), (1, 0), (0, 1), (0, 3), (0, 0)]
    peers = []
    for d_side, d_place in far_first:
        for d_core in range(2):
            if d_side or d_place or d_core:
                peers.append((side + d_side) % 2 * 8 + (place + d_place) % 4 * 2 + (core + d_core) % 2)
    return peers


def cycle_kernel(
    axis_sizes, fields, levels, x_ref, diffusion_ref, coupling_ref, observed_ref, cells_ref, lists_ref, scales_ref, out_ref,
    xs, north, south, grown, blocks, packed, landed, result, returned, weight_ref, total_ref, g_ref, r_ref,
    load_sem, halo_send, halo_recv, block_send, block_recv, back_send, back_recv,
):
    mem, sp = lax.axis_index("mem"), lax.axis_index("sp")
    tiles, bands = axis_sizes
    layers = fields * levels
    groups = layers // 2
    two = 3 * LANES
    members, width = packed.shape[1:]
    peers = peer_order(mem)

    load = pltpu.make_async_copy(x_ref, xs, load_sem)
    load.start()
    barrier = pltpu.get_barrier_semaphore()

    @pl.when(sp > 0)
    def _():
        pl.semaphore_signal(barrier, inc=1, device_id={"sp": sp - 1}, device_id_type=MESH)

    @pl.when(sp < bands - 1)
    def _():
        pl.semaphore_signal(barrier, inc=1, device_id={"sp": sp + 1}, device_id_type=MESH)

    for peer in peers:
        pl.semaphore_signal(barrier, inc=1, device_id={"mem": peer}, device_id_type=MESH)
    pl.semaphore_wait(barrier, tiles - 1 + jnp.minimum(sp, 1) + jnp.minimum(bands - 1 - sp, 1))

    def down(level):
        return pltpu.make_async_remote_copy(
            src_ref=x_ref.at[:, level, :, pl.ds(two, two)], dst_ref=north.at[:, level],
            send_sem=halo_send.at[0, level], recv_sem=halo_recv.at[0, level],
            device_id={"sp": lax.rem(sp + 1, bands)}, device_id_type=MESH,
        )

    def up(level):
        return pltpu.make_async_remote_copy(
            src_ref=x_ref.at[:, level, :, pl.ds(0, two)], dst_ref=south.at[:, level],
            send_sem=halo_send.at[1, level], recv_sem=halo_recv.at[1, level],
            device_id={"sp": lax.rem(sp + bands - 1, bands)}, device_id_type=MESH,
        )

    @pl.loop(0, levels)
    def _(level):
        @pl.when(sp < bands - 1)
        def _():
            down(level).start()

        @pl.when(sp > 0)
        def _():
            up(level).start()

    @pl.when(sp == 0)
    def _():
        north[...] = jnp.zeros_like(north)

    @pl.when(sp == bands - 1)
    def _():
        south[...] = jnp.zeros_like(south)

    weight, total = observation_sums(lists_ref[...], scales_ref[...], observed_ref[...], cells_ref[...], width)
    weight_ref[...] = weight
    total_ref[...] = total
    load.wait()

    inside_north = jnp.minimum(sp, 1).astype(F32)
    inside_south = jnp.minimum(bands - 1 - sp, 1).astype(F32)

    @pl.loop(0, levels)
    def _(level):
        @pl.when(sp > 0)
        def _():
            down(level).wait_recv()

        @pl.when(sp < bands - 1)
        def _():
            up(level).wait_recv()

        diffusion = diffusion_ref[level]
        own = 1.0 - 4.0 * diffusion
        mix = [[coupling_ref[f, g] + own if f == g else coupling_ref[f, g] for g in range(fields)] for f in range(fields)]
        rows = []
        for f in range(fields):
            line = []
            for ref, starts in ((north, (0,)), (xs, (0, two)), (south, (0,))):
                for start in starts:
                    line += row_halves([ref[f, level, :, pl.ds(start + LANES * v, LANES)] for v in range(3)])
            rows.append(line)
        middle = time_step(rows, diffusion, mix)
        for f in range(fields):
            middle[f][0] = tuple(inside_north * v for v in middle[f][0])
            middle[f][-1] = tuple(inside_south * v for v in middle[f][-1])
        final = time_step(middle, diffusion, mix)
        for f in range(fields):
            layer = f * levels + level
            for r in range(len(final[f])):
                grown[0, layer, r] = final[f][r][0]
                grown[1, layer, r] = turn(final[f][r][1], 32)

    @pl.loop(0, groups // 3)
    def _(third):
        for k in range(3):
            group = 3 * third + k
            for half in range(2):
                rows = [grown[half, 2 * group + n // 4, n % 4] for n in range(8)]
                for b, row in enumerate(swap_blocks(rows)):
                    blocks[8 * half + b, group] = row

    def fill(peer, store):
        for quad in range(groups // 4):
            for v, vec in enumerate(pack_four([blocks[peer, 4 * quad + k] for k in range(4)])):
                store(3 * quad + v, vec)
        store(3 * (groups // 4), jnp.where(lane_ids((members, LANES)) < HALF, blocks[peer, groups - 1], 0.0))

    def block_copy(peer, slot):
        return pltpu.make_async_remote_copy(
            src_ref=packed.at[peer], dst_ref=landed.at[slot], send_sem=block_send.at[peer], recv_sem=block_recv.at[slot],
            device_id={"mem": peer}, device_id_type=MESH,
        )

    for peer in peers:

        def store(v, vec):
            packed[peer, :, pl.ds(LANES * v, LANES)] = vec

        fill(peer, store)
        block_copy(peer, mem).start()

    def keep(v, vec):
        landed[mem, :, pl.ds(LANES * v, LANES)] = vec

    fill(mem, keep)
    for peer in peers[::-1]:
        block_copy(peer, peer).wait_recv()

    moved = analyse(landed[...].reshape(tiles * members, width), weight_ref[...], total_ref[...], g_ref, r_ref)
    result[...] = moved.reshape(tiles, members, width)

    def back_copy(peer, slot):
        return pltpu.make_async_remote_copy(
            src_ref=result.at[peer], dst_ref=returned.at[slot], send_sem=back_send.at[peer], recv_sem=back_recv.at[slot],
            device_id={"mem": peer}, device_id_type=MESH,
        )

    for peer in peers:
        back_copy(peer, mem).start()
    for peer in peers:
        block_copy(peer, mem).wait_send()

    @pl.loop(0, levels)
    def _(level):
        @pl.when(sp < bands - 1)
        def _():
            down(level).wait_send()

        @pl.when(sp > 0)
        def _():
            up(level).wait_send()

    def spread_out(ref, owner):
        for quad in range(groups // 4):
            vecs = [ref[owner, :, pl.ds(LANES * (3 * quad + v), LANES)] for v in range(3)]
            for k, part in enumerate(unpack_four(vecs)):
                blocks[owner, 4 * quad + k] = part
        blocks[owner, groups - 1] = ref[owner, :, pl.ds(LANES * 3 * (groups // 4), LANES)]

    spread_out(result, mem)
    for peer in peers[::-1]:
        back_copy(peer, peer).wait_recv()
        spread_out(returned, peer)

    @pl.loop(0, groups // 3)
    def _(third):
        for k in range(3):
            group = 3 * third + k
            halves = [swap_blocks([blocks[8 * half + b, group] for b in range(8)]) for half in range(2)]
            for pair in range(4):
                parts = [halves[n % 2][2 * pair + n // 2] for n in range(4)]
                for v, vec in enumerate(pack_four(parts)):
                    out_ref[2 * group + pair // 2, :, pl.ds(LANES * (3 * (pair % 2) + v), LANES)] = vec

    for peer in peers:
        back_copy(peer, mem).wait_send()


def cycle(x, diffusivity, coupling, observed, cells, lists, scales, axis_sizes):
    fields, levels = coupling.shape[0], diffusivity.shape[0]
    _, _, members, span = x.shape
    layers = fields * levels
    tiles = axis_sizes[0]
    everyone = tiles * members
    width = LANES * (-(-layers * TILE_ROWS * TILE_COLS // LANES))
    vmem, smem = pl.BlockSpec(memory_space=pltpu.VMEM), pl.BlockSpec(memory_space=pltpu.SMEM)
    block = pltpu.VMEM((tiles, members, width), F32)
    halo = pltpu.VMEM((fields, levels, members, 3 * LANES), F32)
    semaphores = pltpu.SemaphoreType.DMA((tiles,))
    return pl.pallas_call(
        functools.partial(cycle_kernel, axis_sizes, fields, levels),
        out_shape=jax.ShapeDtypeStruct((layers, members, span), F32),
        in_specs=[pl.BlockSpec(memory_space=pl.ANY), smem, smem, vmem, vmem, vmem, vmem],
        out_specs=vmem,
        scratch_shapes=[
            pltpu.VMEM((fields, levels, members, span), F32),
            halo,
            halo,
            pltpu.VMEM((2, layers, TILE_ROWS, members, LANES), F32),
            pltpu.VMEM((tiles, layers // 2, members, LANES), F32),
            block,
            block,
            block,
            block,
            pltpu.VMEM((COARSE, width), F32),
            pltpu.VMEM((COARSE, width), F32),
            pltpu.VMEM((COARSE, everyone, everyone), F32),
            pltpu.VMEM((COARSE * PANEL, everyone), F32),
            pltpu.SemaphoreType.DMA,
            pltpu.SemaphoreType.DMA((2, levels)),
            pltpu.SemaphoreType.DMA((2, levels)),
            semaphores,
            semaphores,
            semaphores,
            semaphores,
        ],
        compiler_params=pltpu.CompilerParams(
            collective_id=0, has_side_effects=True, vmem_limit_bytes=56 * 1024 * 1024
        ),
    )(x, diffusivity, coupling, observed, cells, lists, scales)


def on_device(
    axis_sizes,
    cycle_start_state,
    diffusivity,
    coupling,
    observation_value,
    observation_cell,
    observation_lists,
    localization_weight,
):
    members, fields, levels, span = cycle_start_state.shape
    y = cycle(
        cycle_start_state.transpose(1, 2, 0, 3),
        diffusivity,
        coupling,
        observation_value[0],
        observation_cell[0],
        observation_lists[0, 0],
        localization_weight[0, 0],
        axis_sizes,
    )
    return y.reshape(fields, levels, members, span).transpose(2, 0, 1, 3)


def solution(mesh):
    in_specs = (
        P("mem", None, None, "sp"),
        P(),
        P(),
        P("sp", "mem", None),
        P("sp", "mem", None),
        P("sp", "mem", None, None),
        P("sp", "mem", None, None),
    )
    out_specs = P("mem", None, None, "sp")
    axis_sizes = (mesh.shape["mem"], mesh.shape["sp"])
    return jax.shard_map(
        functools.partial(on_device, axis_sizes), mesh=mesh, in_specs=in_specs, out_specs=out_specs, check_vma=False
    )
```

```python
import functools

import jax
import jax.numpy as jnp
from jax import lax
from jax.experimental import pallas as pl
from jax.experimental.pallas import tpu as pltpu
from jax.sharding import PartitionSpec as P

GX = 4
GY = 2
COARSE = 8
PIVOTS = 8
PANEL = 16
F32 = jnp.float32
BF16 = jnp.bfloat16
NT = (((1,), (1,)), ((), ()))
NN = (((1,), (0,)), ((), ()))
TN = (((0,), (0,)), ((), ()))
MESH = pl.DeviceIdType.MESH
LANES = 128
TILE_ROWS = 4
TILE_COLS = 12
HALF = 96


def dot(a, b, dims):
    return lax.dot_general(a, b, dims, preferred_element_type=F32)


def split2(x):
    hi = x.astype(BF16)
    lo = (x - hi.astype(F32)).astype(BF16)
    return hi, lo


def split3(x):
    hi = x.astype(BF16)
    rest = x - hi.astype(F32)
    mid = rest.astype(BF16)
    lo = (rest - mid.astype(F32)).astype(BF16)
    return hi, mid, lo


def observation_sums(lists, scales, observed, cells, lanes):
    nobs = observed.shape[1]
    points, nloc = lists.shape
    pieces = jnp.concatenate(split3(scales), axis=0)
    which = lax.broadcasted_iota(jnp.int32, (nobs, nloc), 0)
    row = lax.broadcasted_iota(jnp.int32, (points, nobs), 0)
    per_obs = jnp.zeros((points, nobs), F32)
    for c in range(points):
        picked = jnp.where(lists[c : c + 1, :] == which, 1.0, 0.0).astype(BF16)
        got = dot(pieces, picked, NT)
        got = got[:points] + got[points : 2 * points] + got[2 * points :]
        per_obs = jnp.where(row == c, got, per_obs)
    both = jnp.concatenate(split3(per_obs) + split3(per_obs * observed), axis=0)
    place = lax.broadcasted_iota(jnp.int32, (lanes, nobs), 0)
    spots = jnp.where(cells == place, 1.0, 0.0).astype(BF16)
    got = dot(both, spots, NT)
    p = points
    weight = got[:p] + got[p : 2 * p] + got[2 * p : 3 * p]
    total = got[3 * p : 4 * p] + got[4 * p : 5 * p] + got[5 * p :]
    return weight, total


def factor_inverses(g_ref, r_ref):
    p, members, _ = g_ref.shape
    lane = lax.broadcasted_iota(jnp.int32, (p, members), 1)
    panel_lane = lax.broadcasted_iota(jnp.int32, (PANEL, members), 1)
    panel_row = lax.broadcasted_iota(jnp.int32, (PANEL, members), 0)

    def spread(v, i):
        return jnp.broadcast_to(v[:, i : i + 1], v.shape)

    for b0 in range(0, members, PANEL):
        for c in range(p):
            r_ref[pl.ds(c, PANEL, stride=p), :] = g_ref[c, pl.ds(b0, PANEL), :]
        for k0 in range(0, PANEL, PIVOTS):
            at = b0 + k0
            rows = [r_ref[pl.ds(p * (k0 + t), p), :] for t in range(PIVOTS)]
            e = [[spread(rows[t], at + s) for t in range(s + 1)] for s in range(PIVOTS)]
            block = (lane >= at) & (lane < at + PIVOTS)
            rows = [jnp.where(block, jnp.where(lane == at + t, 1.0, 0.0), rows[t]) for t in range(PIVOTS)]
            for t in range(PIVOTS):
                inverse = 1.0 / e[t][t]
                for s in range(t + 1, PIVOTS):
                    ratio = e[s][t] * inverse
                    for j in range(t + 1, s + 1):
                        e[s][j] = e[s][j] - ratio * e[j][t]
                    rows[s] = rows[s] - ratio * rows[t]
            done = [rows[t] * lax.rsqrt(e[t][t]) for t in range(PIVOTS)]
            for t in range(PIVOTS):
                r_ref[pl.ds(p * (k0 + t), p), :] = done[t]
            for i in range(k0 + PIVOTS, PANEL):
                acc = jnp.where(block, 0.0, r_ref[pl.ds(p * i, p), :])
                for t in range(PIVOTS):
                    acc = acc - spread(done[t], b0 + i) * done[t]
                r_ref[pl.ds(p * i, p), :] = acc
        end = b0 + PANEL
        for c in range(p):
            v = r_ref[pl.ds(c, PANEL, stride=p), :]
            lower = panel_lane <= panel_row + b0
            g_ref[c, pl.ds(b0, PANEL), :] = jnp.where(lower, v, 0.0)
            if end < members:
                hi, mid, lo = split3(v)
                kept = jnp.where(lower | (panel_lane >= end), 1.0, 0.0).astype(BF16)
                k_hi, k_mid, k_lo = hi * kept, mid * kept, lo * kept
                left = jnp.concatenate([hi, hi, mid, hi, mid, lo], axis=0)
                right = jnp.concatenate([k_hi, k_mid, k_hi, k_lo, k_mid, k_hi], axis=0)
                change = dot(left[:, end:] if end % 128 == 0 else left, right, TN)
                below = g_ref[c, pl.ds(end, members - end), :]
                low_lane = lax.broadcasted_iota(jnp.int32, below.shape, 1)
                below = jnp.where((low_lane >= b0) & (low_lane < end), 0.0, below)
                g_ref[c, pl.ds(end, members - end), :] = below - change[end:, :]


def lane_ids(shape):
    return lax.broadcasted_iota(jnp.int32, shape, len(shape) - 1)


def turn(x, shift):
    return pltpu.roll(x, shift % LANES, x.ndim - 1)


def swap_blocks(rows):
    rows = list(rows)
    lane = lane_ids(rows[0].shape)
    edge = [TILE_COLS * k for k in range(9)]
    between = [(lane >= edge[k]) & (lane < edge[k + 1]) for k in range(8)]
    keeps = {
        4: lane < edge[4],
        2: (lane < edge[2]) | ((lane >= edge[4]) & (lane < edge[6])),
        1: (between[0] | between[2]) | (between[4] | between[6]),
    }
    for step in (4, 2, 1):
        width = TILE_COLS * step
        keep = keeps[step]
        for a in range(8):
            if a & step:
                continue
            low, high = rows[a], rows[a + step]
            rows[a] = jnp.where(keep, low, turn(high, width))
            rows[a + step] = jnp.where(keep, turn(low, -width), high)
    return rows


def pack_four(parts):
    lane = lane_ids(parts[0].shape)
    one, two, three = turn(parts[1], 96), turn(parts[2], 64), turn(parts[3], 32)
    return [
        jnp.where(lane < 96, parts[0], one),
        jnp.where(lane < 64, one, two),
        jnp.where(lane < 32, two, three),
    ]


def unpack_four(vecs):
    lane = lane_ids(vecs[0].shape)
    return [
        vecs[0],
        turn(jnp.where(lane < 64, vecs[1], vecs[0]), -96),
        turn(jnp.where(lane < 64, vecs[2], vecs[1]), -64),
        turn(vecs[2], -32),
    ]


def row_halves(vecs):
    lane = lane_ids(vecs[0].shape)
    first, middle, last = vecs
    return [
        (first, jnp.where(lane < 64, middle, first)),
        (turn(jnp.where(lane < 64, last, middle), 64), turn(last, 64)),
    ]


def time_step(rows, diffusion, mix):
    fields, count = len(rows), len(rows[0])
    lane = lane_ids(rows[0][0][0].shape)
    out = [[None] * (count - 2) for _ in range(fields)]
    for r in range(1, count - 1):
        pair = [[None, None] for _ in range(fields)]
        for h in range(2):
            for f in range(fields):
                center = rows[f][r][h]
                before, after = turn(center, 1), turn(center, -1)
                if h == 0:
                    before = jnp.where(lane == 0, 0.0, before)
                else:
                    after = jnp.where(lane == 63, 0.0, after)
                around = (rows[f][r - 1][h] + rows[f][r + 1][h]) + (before + after)
                new = diffusion * around
                for g in range(fields):
                    new = new + mix[f][g] * rows[g][r][h]
                pair[f][h] = new
        for f in range(fields):
            out[f][r - 1] = tuple(pair[f])
    return out


def regrouped(cells, fields, levels):
    spots = TILE_ROWS * TILE_COLS
    layer, spot = lax.div(cells, spots), lax.rem(cells, spots)
    field, level = lax.div(layer, levels), lax.rem(layer, levels)
    return (lax.div(level, 2) * fields + field) * (2 * spots) + lax.rem(level, 2) * spots + spot


def hat_rows(lanes):
    lane = lax.broadcasted_iota(jnp.int32, (1, lanes), 1) % (TILE_ROWS * TILE_COLS)
    row, col = (lane // TILE_COLS).astype(F32), (lane % TILE_COLS).astype(F32)
    span_y, span_x = (TILE_ROWS - 1) / (GY - 1), (TILE_COLS - 1) / (GX - 1)
    hat_y = [jnp.maximum(0.0, 1.0 - jnp.abs(row - i * span_y) / span_y) for i in range(GY)]
    hat_x = [jnp.maximum(0.0, 1.0 - jnp.abs(col - j * span_x) / span_x) for j in range(GX)]
    return [y * x for y in hat_y for x in hat_x]


def analyse(field, weight, total, g_ref, r_ref):
    members, lanes = field.shape
    p = COARSE
    mean = jnp.sum(field, axis=0, keepdims=True) * (1.0 / members)
    dev = field - mean
    hi, mid, lo = split3(dev)
    both = jnp.concatenate([hi, mid], axis=0)
    lead = float(members - 1)
    eye = jnp.where(
        lax.broadcasted_iota(jnp.int32, (members, members), 0) == lax.broadcasted_iota(jnp.int32, (members, members), 1),
        lead,
        0.0,
    )
    stack = 4
    for c0 in range(0, p, stack):
        thirds = [split3(dev * weight[c : c + 1, :]) for c in range(c0, c0 + stack)]
        s_hi, s_mid, s_lo = [jnp.concatenate([third[k] for third in thirds], axis=0) for k in range(3)]
        g = dot(jnp.concatenate([s_hi, s_mid], axis=0), both, NT)
        g = g[: stack * members] + g[stack * members :]
        g = g[:, :members] + g[:, members:] + (dot(s_hi, lo, NT) + dot(s_lo, hi, NT))
        for k in range(stack):
            g_ref[c0 + k] = g[members * k : members * (k + 1)] + eye
    gap = total - mean * weight
    g_hi, g_mid, g_lo = split3(gap)
    pull = dot(g_hi, both, NT) + dot(g_mid, both, NT)
    pull = pull[:, :members] + pull[:, members:] + (dot(g_hi, lo, NT) + dot(g_lo, hi, NT))

    factor_inverses(g_ref, r_ref)

    ws = []
    for c in range(p):
        m = g_ref[c]
        y = jnp.sum(m * pull[c : c + 1, :], axis=1, keepdims=True)
        ws.append(jnp.sum(m * y, axis=0, keepdims=True))
    return mean, both, hi, ws, hat_rows(lanes)


def blend(parts, start, count, g_ref):
    mean, both, hi, ws, hats = parts
    root = float(hi.shape[0] - 1) ** 0.5
    pairs = [split2(g_ref[c, pl.ds(start, count), :] * root + ws[c]) for c in range(COARSE)]
    high = jnp.concatenate([w_hi for w_hi, _ in pairs], axis=0)
    low = jnp.concatenate([w_lo for _, w_lo in pairs], axis=0)
    product = dot(jnp.concatenate([high, high], axis=1), both, NN) + dot(low, hi, NN)
    moved = mean
    for c in range(COARSE):
        moved = moved + hats[c] * product[count * c : count * (c + 1)]
    return moved


def peer_order(mem):
    side, place, core = mem // 8, mem // 2 % 4, mem % 2
    far_first = [(1, 2), (1, 1), (1, 3), (1, 0), (0, 2), (0, 1), (0, 3), (0, 0)]
    peers = []
    for d_side, d_place in far_first:
        for d_core in range(2):
            if d_side or d_place or d_core:
                peers.append((side + d_side) % 2 * 8 + (place + d_place) % 4 * 2 + (core + d_core) % 2)
    return peers


def cycle_kernel(
    axis_sizes, fields, levels, x_ref, diffusion_ref, coupling_ref, observed_ref, cells_ref, lists_ref, scales_ref, out_ref,
    xs, north, south, grown, blocks, packed, landed, result, returned, weight_ref, total_ref, g_ref, r_ref,
    load_sem, halo_send, halo_recv, block_send, block_recv, back_send, back_recv,
):
    mem, sp = lax.axis_index("mem"), lax.axis_index("sp")
    tiles, bands = axis_sizes
    layers = fields * levels
    groups = layers // 2
    two = 3 * LANES
    members, width = packed.shape[1:]
    peers = peer_order(mem)

    load = pltpu.make_async_copy(x_ref, xs, load_sem)
    load.start()
    barrier = pltpu.get_barrier_semaphore()

    @pl.when(sp > 0)
    def _():
        pl.semaphore_signal(barrier, inc=1, device_id={"sp": sp - 1}, device_id_type=MESH)

    @pl.when(sp < bands - 1)
    def _():
        pl.semaphore_signal(barrier, inc=1, device_id={"sp": sp + 1}, device_id_type=MESH)

    for peer in peers:
        pl.semaphore_signal(barrier, inc=1, device_id={"mem": peer}, device_id_type=MESH)
    pl.semaphore_wait(barrier, tiles - 1 + jnp.minimum(sp, 1) + jnp.minimum(bands - 1 - sp, 1))

    def down(level):
        return pltpu.make_async_remote_copy(
            src_ref=x_ref.at[:, level, :, pl.ds(two, two)], dst_ref=north.at[:, level],
            send_sem=halo_send.at[0, level], recv_sem=halo_recv.at[0, level],
            device_id={"sp": lax.rem(sp + 1, bands)}, device_id_type=MESH,
        )

    def up(level):
        return pltpu.make_async_remote_copy(
            src_ref=x_ref.at[:, level, :, pl.ds(0, two)], dst_ref=south.at[:, level],
            send_sem=halo_send.at[1, level], recv_sem=halo_recv.at[1, level],
            device_id={"sp": lax.rem(sp + bands - 1, bands)}, device_id_type=MESH,
        )

    @pl.loop(0, levels)
    def _(level):
        @pl.when(sp < bands - 1)
        def _():
            down(level).start()

        @pl.when(sp > 0)
        def _():
            up(level).start()

    @pl.when(sp == 0)
    def _():
        north[...] = jnp.zeros_like(north)

    @pl.when(sp == bands - 1)
    def _():
        south[...] = jnp.zeros_like(south)

    load.wait()

    inside_north = jnp.minimum(sp, 1).astype(F32)
    inside_south = jnp.minimum(bands - 1 - sp, 1).astype(F32)

    def advance(level):
        @pl.when(sp > 0)
        def _():
            down(level).wait_recv()

        @pl.when(sp < bands - 1)
        def _():
            up(level).wait_recv()

        diffusion = diffusion_ref[level]
        own = 1.0 - 4.0 * diffusion
        mix = [[coupling_ref[f, g] + own if f == g else coupling_ref[f, g] for g in range(fields)] for f in range(fields)]
        rows = []
        for f in range(fields):
            line = []
            for ref, starts in ((north, (0,)), (xs, (0, two)), (south, (0,))):
                for start in starts:
                    line += row_halves([ref[f, level, :, pl.ds(start + LANES * v, LANES)] for v in range(3)])
            rows.append(line)
        middle = time_step(rows, diffusion, mix)
        for f in range(fields):
            middle[f][0] = tuple(inside_north * v for v in middle[f][0])
            middle[f][-1] = tuple(inside_south * v for v in middle[f][-1])
        final = time_step(middle, diffusion, mix)
        for f in range(fields):
            layer = f * levels + level
            for r in range(len(final[f])):
                grown[0, layer, r] = final[f][r][0]
                grown[1, layer, r] = turn(final[f][r][1], 32)

    def regroup(pair):
        for f in range(fields):
            for half in range(2):
                rows = [grown[half, f * levels + 2 * pair + n // 4, n % 4] for n in range(8)]
                for b, row in enumerate(swap_blocks(rows)):
                    blocks[8 * half + b, fields * pair + f] = row

    def packed_vector(peer, v):
        lane = lane_ids((members, LANES))
        quad, j = v // 3, v % 3
        first = blocks[peer, 4 * quad + j]
        if 4 * quad + j + 1 == groups:
            return jnp.where(lane < HALF, first, 0.0)
        second = turn(blocks[peer, 4 * quad + j + 1], HALF - 32 * j)
        return jnp.where(lane < HALF - 32 * j, turn(first, -32 * j) if j else first, second)

    def block_copy(part, peer, slot):
        lanes = pl.ds(LANES * cuts[part], LANES * (cuts[part + 1] - cuts[part]))
        return pltpu.make_async_remote_copy(
            src_ref=packed.at[peer, :, lanes], dst_ref=landed.at[slot, :, lanes],
            send_sem=block_send.at[part, peer], recv_sem=block_recv.at[part, slot],
            device_id={"mem": peer}, device_id_type=MESH,
        )

    cuts = (0, 4, width // LANES)
    bounds = (0, 2, levels // 2)
    for part in range(2):
        pl.loop(2 * bounds[part], 2 * bounds[part + 1])(advance)
        pl.loop(bounds[part], bounds[part + 1])(regroup)
        for peer in peers:
            for v in range(cuts[part], cuts[part + 1]):
                packed[peer, :, pl.ds(LANES * v, LANES)] = packed_vector(peer, v)
            block_copy(part, peer, mem).start()
        for v in range(cuts[part], cuts[part + 1]):
            landed[mem, :, pl.ds(LANES * v, LANES)] = packed_vector(mem, v)
    places = regrouped(cells_ref[...], fields, levels)
    weight, total = observation_sums(lists_ref[...], scales_ref[...], observed_ref[...], places, width)
    weight_ref[...] = weight
    total_ref[...] = total
    for part in range(2):
        for peer in peers[::-1]:
            block_copy(part, peer, peer).wait_recv()

    parts = analyse(landed[...].reshape(tiles * members, width), weight_ref[...], total_ref[...], g_ref, r_ref)

    def back_copy(peer, slot):
        return pltpu.make_async_remote_copy(
            src_ref=result.at[peer], dst_ref=returned.at[slot], send_sem=back_send.at[peer], recv_sem=back_recv.at[slot],
            device_id={"mem": peer}, device_id_type=MESH,
        )

    side = tiles // 2
    for turn_to in range(2):
        first = side * ((mem // side + 1 + turn_to) % 2)
        moved = blend(parts, pl.multiple_of(members * first, members * side), members * side, g_ref)
        result[pl.ds(first, side)] = moved.reshape(side, members, width)
        for peer in peers[:side] if turn_to == 0 else peers[side:]:
            back_copy(peer, mem).start()
    for part in range(2):
        for peer in peers:
            block_copy(part, peer, mem).wait_send()

    @pl.loop(0, levels)
    def _(level):
        @pl.when(sp < bands - 1)
        def _():
            down(level).wait_send()

        @pl.when(sp > 0)
        def _():
            up(level).wait_send()

    def spread_out(ref, owner):
        for quad in range(groups // 4):
            vecs = [ref[owner, :, pl.ds(LANES * (3 * quad + v), LANES)] for v in range(3)]
            for k, part in enumerate(unpack_four(vecs)):
                blocks[owner, 4 * quad + k] = part
        blocks[owner, groups - 1] = ref[owner, :, pl.ds(LANES * 3 * (groups // 4), LANES)]

    spread_out(result, mem)
    for peer in peers[::-1]:
        back_copy(peer, peer).wait_recv()
        spread_out(returned, peer)

    @pl.loop(0, levels // 2)
    def _(pair):
        for f in range(fields):
            group = fields * pair + f
            halves = [swap_blocks([blocks[8 * half + b, group] for b in range(8)]) for half in range(2)]
            for two_rows in range(4):
                parts = [halves[n % 2][2 * two_rows + n // 2] for n in range(4)]
                for v, vec in enumerate(pack_four(parts)):
                    layer = f * levels + 2 * pair + two_rows // 2
                    out_ref[layer, :, pl.ds(LANES * (3 * (two_rows % 2) + v), LANES)] = vec

    for peer in peers:
        back_copy(peer, mem).wait_send()


def cycle(x, diffusivity, coupling, observed, cells, lists, scales, axis_sizes):
    fields, levels = coupling.shape[0], diffusivity.shape[0]
    _, _, members, span = x.shape
    layers = fields * levels
    tiles = axis_sizes[0]
    everyone = tiles * members
    width = LANES * (-(-layers * TILE_ROWS * TILE_COLS // LANES))
    vmem, smem = pl.BlockSpec(memory_space=pltpu.VMEM), pl.BlockSpec(memory_space=pltpu.SMEM)
    block = pltpu.VMEM((tiles, members, width), F32)
    halo = pltpu.VMEM((fields, levels, members, 3 * LANES), F32)
    semaphores = pltpu.SemaphoreType.DMA((tiles,))
    return pl.pallas_call(
        functools.partial(cycle_kernel, axis_sizes, fields, levels),
        out_shape=jax.ShapeDtypeStruct((layers, members, span), F32),
        in_specs=[pl.BlockSpec(memory_space=pl.ANY), smem, smem, vmem, vmem, vmem, vmem],
        out_specs=vmem,
        scratch_shapes=[
            pltpu.VMEM((fields, levels, members, span), F32),
            halo,
            halo,
            pltpu.VMEM((2, layers, TILE_ROWS, members, LANES), F32),
            pltpu.VMEM((tiles, layers // 2, members, LANES), F32),
            block,
            block,
            block,
            block,
            pltpu.VMEM((COARSE, width), F32),
            pltpu.VMEM((COARSE, width), F32),
            pltpu.VMEM((COARSE, everyone, everyone), F32),
            pltpu.VMEM((COARSE * PANEL, everyone), F32),
            pltpu.SemaphoreType.DMA,
            pltpu.SemaphoreType.DMA((2, levels)),
            pltpu.SemaphoreType.DMA((2, levels)),
            pltpu.SemaphoreType.DMA((2, tiles)),
            pltpu.SemaphoreType.DMA((2, tiles)),
            semaphores,
            semaphores,
        ],
        compiler_params=pltpu.CompilerParams(
            collective_id=0, has_side_effects=True, vmem_limit_bytes=56 * 1024 * 1024
        ),
    )(x, diffusivity, coupling, observed, cells, lists, scales)


def on_device(
    axis_sizes,
    cycle_start_state,
    diffusivity,
    coupling,
    observation_value,
    observation_cell,
    observation_lists,
    localization_weight,
):
    members, fields, levels, span = cycle_start_state.shape
    y = cycle(
        cycle_start_state.transpose(1, 2, 0, 3),
        diffusivity,
        coupling,
        observation_value[0],
        observation_cell[0],
        observation_lists[0, 0],
        localization_weight[0, 0],
        axis_sizes,
    )
    return y.reshape(fields, levels, members, span).transpose(2, 0, 1, 3)


def solution(mesh):
    in_specs = (
        P("mem", None, None, "sp"),
        P(),
        P(),
        P("sp", "mem", None),
        P("sp", "mem", None),
        P("sp", "mem", None, None),
        P("sp", "mem", None, None),
    )
    out_specs = P("mem", None, None, "sp")
    axis_sizes = (mesh.shape["mem"], mesh.shape["sp"])
    return jax.shard_map(
        functools.partial(on_device, axis_sizes), mesh=mesh, in_specs=in_specs, out_specs=out_specs, check_vma=False
    )
```
